256 devices in a mesh: dp: 16 (over z, y_hi), mp: 16 (over x, y_lo, core).
Axes of the slice: x: 4, y: 4 (y_hi: 2, y_lo: 2; y = y_hi * 2 + y_lo), z: 8, core: 2. Of those that a mesh axis runs over, the one named last changes fastest.
Arguments:
- tokens: bfloat16 [8192, 6144], P(('dp', 'mp')), may hold values from -24 to 24
- w_qkv: bfloat16 [6144, 32, 384], P(None, 'mp'), may hold values from -0.078125 to 0.078125
- w_out: bfloat16 [6144, 32, 128], P('dp', 'mp'), may hold values from -0.09375 to 0.09375
- grad_out: bfloat16 [8192, 6144], P(('dp', 'mp')), may hold values from -24 to 24
Outputs:
- grad_wqkv: bfloat16 [6144, 32, 384], P('dp', 'mp')
- grad_wout: bfloat16 [6144, 32, 128], P('dp', 'mp')
The draws below stay inside these ranges and needn't reach their ends.
All inputs are finite; a program needn't handle non-finite values.
Results may differ from the reference program's by a relative error of at most 0.02.
Values may be sent and summed in bfloat16 or wider, within the bound.
A program may use at most 128 MiB of HBM per device.

```python
import jax
import jax.numpy as jnp
from jax import lax

D = 6144
H = 32
HD = 128
PATCH = 256
IMAGES = 32
TOKENS = 8192
N_DP = 16


def raised(array, own_key, source, target, blocks, factor):
    def block_of(dim):
        return (jnp.arange(array.shape[dim]) // (array.shape[dim] // blocks)).reshape((-1,) + (1,) * (array.ndim - 1 - dim))

    near = jax.random.permutation(own_key, blocks)[block_of(target)]
    second = (block_of(target) + blocks // 2) % blocks
    return jnp.where((block_of(source) == near) | (block_of(source) == second), factor * array, array)


def level_of(stream_key, dims, shards, least, high):
    loudness = 1.0
    for position, shards_of in shards:
        steps = jax.random.uniform(jax.random.fold_in(jax.random.fold_in(stream_key, 6), position), (shards_of,), jnp.float32, least / len(shards), high / len(shards))
        loudness = loudness * jnp.repeat(jnp.exp(steps), dims[position] // shards_of).reshape((-1,) + (1,) * (len(dims) - 1 - position))
    return loudness


def gaussian(rng, extent, width, limit, split=(), held_as=jnp.bfloat16):
    entries = width * jax.random.normal(rng, extent, jnp.float32)
    if split:
        entries = entries * level_of(rng, extent, split, -0.22, 0.18)
    return jnp.clip(entries, -limit, limit).astype(held_as)


def noise_with(stream_key, shape, scale, bound, cuts, heavy, kind=jnp.bfloat16):
    result = scale * jax.random.normal(stream_key, shape, jnp.float32)
    if cuts:
        result = result * level_of(stream_key, shape, cuts, -0.22, 0.18)
    return jnp.clip(raised(result, jax.random.fold_in(stream_key, 3), *heavy), -bound, bound).astype(kind)


def setup_inputs(seed: int = 0) -> dict:
    key_list = jax.random.split(jax.random.key(seed), 5)
    tokens = noise_with(key_list[0], (TOKENS, D), 1.0, 24.0, ((0, 256),), (0, 1, 256, 6.0))
    w_qkv = gaussian(key_list[1], (D, H, 3 * HD), D ** -0.5, 0.078125, ((1, 16),))
    w_out = gaussian(key_list[2], (D, H, HD), (H * HD) ** -0.5, 0.09375, ((0, 16), (1, 16)))
    grad_out = noise_with(key_list[3], (TOKENS, D), 1.0, 24.0, ((0, 256),), (0, 1, 256, 6.0))
    return dict(tokens=tokens, w_qkv=w_qkv, w_out=w_out, grad_out=grad_out)


def layer_norm(values):
    average = lax.optimization_barrier(jnp.mean(values, axis=-1, keepdims=True))
    centred = values - average
    spread = lax.optimization_barrier(jnp.mean(centred * centred, axis=-1, keepdims=True))
    return centred * lax.rsqrt(spread + 1e-06)

def widen(values):
    return values.astype(jnp.float32)

def reference(tokens, w_qkv, w_out, grad_out):
    factor = HD ** (-0.5)
    projected = jnp.einsum('td,dhe->the', widen(tokens), widen(w_qkv))
    query_raw = projected[..., :HD]
    key_raw = projected[..., HD:2 * HD]
    query_hat = layer_norm(query_raw).astype(jnp.bfloat16)
    key_hat = layer_norm(key_raw).astype(jnp.bfloat16)
    value_hat = projected[..., 2 * HD:].astype(jnp.bfloat16)

    def images(values):
        return widen(values).reshape(IMAGES, PATCH, H, HD)
    scores = jnp.einsum('iqhe,ikhe->ihqk', images(query_hat), images(key_hat)) * factor
    weights = jnp.exp(scores)
    chances = weights / lax.optimization_barrier(jnp.sum(weights, axis=-1, keepdims=True))
    chances_low = widen(chances.astype(jnp.bfloat16))
    context = jnp.einsum('ihqk,ikhe->iqhe', chances_low, images(value_hat)).reshape(TOKENS, H, HD).astype(jnp.bfloat16)
    grad_context = jnp.einsum('td,dhe->the', widen(grad_out), widen(w_out)).astype(jnp.bfloat16)
    grad_chances = jnp.einsum('iqhe,ikhe->ihqk', images(grad_context), images(value_hat))
    grad_value = jnp.einsum('ihqk,iqhe->ikhe', chances_low, images(grad_context)).reshape(TOKENS, H, HD)
    grad_scores = chances * (grad_chances - lax.optimization_barrier(jnp.sum(chances * grad_chances, axis=-1, keepdims=True))) * factor
    scores_low = widen(grad_scores.astype(jnp.bfloat16))
    grad_qhat = jnp.einsum('ihqk,ikhe->iqhe', scores_low, images(key_hat)).reshape(TOKENS, H, HD)
    grad_khat = jnp.einsum('ihqk,iqhe->ikhe', scores_low, images(query_hat)).reshape(TOKENS, H, HD)
    grad_query = jax.vjp(layer_norm, query_raw)[1](grad_qhat)[0]
    grad_key = jax.vjp(layer_norm, key_raw)[1](grad_khat)[0]
    grad_proj = jnp.concatenate([grad_query, grad_key, grad_value], axis=-1).astype(jnp.bfloat16)
    group_rows = TOKENS // N_DP

    def add_group(running, inputs):
        tok_part, proj_part, out_part, ctx_part = inputs
        term_qkv = jnp.einsum('td,the->dhe', widen(tok_part), widen(proj_part))
        term_out = jnp.einsum('td,the->dhe', widen(out_part), widen(ctx_part))
        joined = jnp.concatenate([term_qkv, term_out], axis=-1)
        rounded = lax.optimization_barrier(joined.astype(jnp.bfloat16))
        return (running + widen(rounded), None)
    start_zero = jnp.zeros((D, H, 4 * HD), jnp.float32)
    summed, unused = lax.scan(add_group, start_zero, (tokens.reshape(N_DP, group_rows, D), grad_proj.reshape(N_DP, group_rows, H, 3 * HD), grad_out.reshape(N_DP, group_rows, D), context.reshape(N_DP, group_rows, H, HD)))
    return (summed[..., :3 * HD].astype(jnp.bfloat16), summed[..., 3 * HD:].astype(jnp.bfloat16))
```

```python
import jax
import jax.numpy as jnp
from jax import lax
from jax.experimental import pallas as pl
from jax.experimental.pallas import tpu as pltpu
from jax.sharding import PartitionSpec as P

MESH = pl.DeviceIdType.MESH
F32 = jnp.float32
BF16 = jnp.bfloat16

NX, NZ = 4, 8
BLOCK = 32
PATCH = 256
WIDTH = 6144
SPAN = 384
PAIR = 2 * SPAN
ROUNDS = 2 * NZ
HD = 128
EPS = 1e-06
FACTOR = HD ** (-0.5)


def dot(a, b, dims):
    return lax.dot_general(a, b, (dims, ((), ())), preferred_element_type=F32)


def centre(values):
    centred = values - jnp.mean(values, axis=-1, keepdims=True)
    spread = jnp.mean(centred * centred, axis=-1, keepdims=True)
    return centred, lax.rsqrt(spread + EPS)


def norm_grad(centred, scale, grad):
    slope = jnp.mean(grad * centred, axis=-1, keepdims=True) * (scale * scale * scale)
    inner = grad * scale - centred * slope
    return inner - jnp.mean(inner, axis=-1, keepdims=True)


def kernel(
    tok_ref, wq_ref, wo_ref, go_ref,
    oq_ref, oc_ref,
    rows, extra, wq, wo, wpart, proj, gctx, hats, chances, bt, run, first,
    local, g_send, g_recv, w_send, w_recv, y_send, y_recv, b_send, b_recv, r_send, r_recv,
):
    dp, mp = lax.axis_index("dp"), lax.axis_index("mp")
    z, yh = dp // 2, dp % 2
    x, yl, core = mp // 4, (mp // 2) % 2, mp % 2

    def place(z_, yh_, x_, yl_, core_):
        return (z_ * 2 + yh_, x_ * 4 + yl_ * 2 + core_)

    right_x, left_x, far_x = (x + 1) % NX, (x + 3) % NX, (x + 2) % NX
    pair = place(z, yh, x, 1 - yl, core)
    right = place(z, yh, right_x, yl, core)
    left = place(z, yh, left_x, yl, core)
    sibling = place(z, yh, x, yl, 1 - core)
    outer = place(z, 1 - yh, x, 1 - yl, core)
    across = place(z, 1 - yh, x, yl, core)
    up = place((z + 1) % NZ, yh, x, yl, core)
    down = place((z + 7) % NZ, yh, x, yl, core)
    sides = (up, down)

    def remote(src, dst, send, recv, to):
        return pltpu.make_async_remote_copy(
            src_ref=src, dst_ref=dst, send_sem=send, recv_sem=recv, device_id=to, device_id_type=MESH
        )

    barrier = pltpu.get_barrier_semaphore()
    for to in (pair, right, left, sibling, outer, across, up, down):
        pl.semaphore_signal(barrier, inc=1, device_id=to, device_id_type=MESH)

    mine = x * 2 + yl
    loads = (
        pltpu.make_async_copy(tok_ref, rows.at[0, mine, core], local.at[0]),
        pltpu.make_async_copy(go_ref, rows.at[1, mine, core], local.at[1]),
        pltpu.make_async_copy(wo_ref, wo.at[z, yh], local.at[2]),
        pltpu.make_async_copy(wq_ref, wq, local.at[3]),
    )
    for load in loads:
        load.start()
    proj[...] = jnp.zeros_like(proj)
    gctx[...] = jnp.zeros_like(gctx)
    for load in loads[:3]:
        load.wait()
    pl.semaphore_wait(barrier, 8)


    def target(r):
        j = r % NZ
        step = NZ // 2 - (j + 1) // 2
        return (z + jnp.where(j % 2 == 1, step, NZ - step)) % NZ

    def columns(r):
        return pl.ds(pl.multiple_of(target(r) * PAIR, PAIR), PAIR)

    def block(r, bx, by):
        return rows.at[r // NZ, bx * 2 + by, core, :, columns(r)]

    def move(r, slot, bx, by, to):
        part = block(r, bx, by)
        return remote(part, part, g_send.at[r, slot], g_recv.at[r, slot], to)

    def landed(r, slot, bx, by):
        move(r, slot, bx, by, pair).wait_recv()

    def swap(r, lane):
        part = rows.at[r // NZ, :, lane, :, columns(r)]
        return remote(part, part, g_send.at[r, 7], g_recv.at[r, 7], sibling)

    def lend(r):
        cols = pl.ds(pl.multiple_of(target(r) * PAIR + (1 - yh) * SPAN, SPAN), SPAN)
        there = pl.ds(pl.multiple_of(target(r) * SPAN, SPAN), SPAN)
        half = pl.ds(core * 4, 4)
        return remote(
            rows.at[r // NZ, half, :, :, cols], extra.at[r // NZ, half, :, :, there],
            g_send.at[r, 8], g_recv.at[r, 8], outer,
        )

    def share(r, owner):
        there = pl.ds(pl.multiple_of(target(r) * SPAN, SPAN), SPAN)
        part = extra.at[r // NZ, pl.ds(owner * 4, 4), :, :, there]
        return remote(part, part, g_send.at[r, 9], g_recv.at[r, 9], sibling)


    def weights(side, m):
        hop = m // 2
        from_z = (z + (NZ - hop if side == 0 else hop)) % NZ
        own = (m % 2 == 0) if (m < 6 or side == 0) else False
        part = wo.at[from_z, yh if own else 1 - yh]
        return remote(part, part, w_send.at[side, m], w_recv.at[side, m], sides[side])

    def weights_landed(m):
        for side in range(2):
            weights(side, m).wait_recv()

    def weights_across():
        part = wo.at[z, yh]
        return remote(part, part, y_send.at[0], y_recv.at[0], across)

    def send_weights(m):
        if m == 1:
            weights_across().wait_recv()
        if m >= 2:
            weights_landed(m - 2)
        if m == 6:
            weights_landed(5)
        for side in range(2):
            weights(side, m).start()


    def image_rows(i):
        return pl.ds(pl.multiple_of(i * PATCH, PATCH), PATCH)

    def head_part(i, h, part):
        return proj[image_rows(i), pl.ds(pl.multiple_of((h * 3 + part) * HD, HD), HD)]

    def sums(g, h):
        return pl.ds(pl.multiple_of((g * 2 + h) * HD, HD), HD)

    def hand_over(g, n):
        i, h = n // 2, n % 2
        return remote(
            bt.at[0, sums(g, h), image_rows(i)], bt.at[1, sums(g, h), image_rows(i)],
            b_send.at[g, n], b_recv.at[g, n], across,
        )

    def forward(n):
        i, h = n // 2, n % 2
        centred_q, scale_q = centre(head_part(i, h, 0))
        centred_k, scale_k = centre(head_part(i, h, 1))
        query_hat = (centred_q * scale_q).astype(BF16)
        key_hat = (centred_k * scale_k).astype(BF16)
        value_hat = head_part(i, h, 2).astype(BF16)
        hats[n, 0] = query_hat
        hats[n, 1] = key_hat
        weight = jnp.exp(dot(query_hat, key_hat, ((1,), (1,))) * FACTOR)
        chance = weight / jnp.sum(weight, axis=-1, keepdims=True)
        chances[n] = chance
        context = dot(chance.astype(BF16), value_hat, ((1,), (0,)))
        bt[0, sums(3, h), image_rows(i)] = context.T.astype(BF16)
        hand_over(3, n).start()

    def backward(n):
        i, h = n // 2, n % 2
        chance = chances[n]
        chance_low = chance.astype(BF16)
        query_hat, key_hat = hats[n, 0], hats[n, 1]
        value_hat = head_part(i, h, 2).astype(BF16)
        grad_context = gctx[image_rows(i), pl.ds(pl.multiple_of(h * HD, HD), HD)].astype(BF16)
        grad_value = dot(chance_low, grad_context, ((0,), (0,)))
        bt[0, sums(0, h), image_rows(i)] = grad_value.T.astype(BF16)
        hand_over(0, n).start()
        grad_chance = dot(grad_context, value_hat, ((1,), (1,)))
        inner = jnp.sum(chance * grad_chance, axis=-1, keepdims=True)
        grad_score = (chance * (grad_chance - inner) * FACTOR).astype(BF16)
        grad_qhat = dot(grad_score, key_hat, ((1,), (0,)))
        grad_khat = dot(grad_score, query_hat, ((0,), (0,)))
        grad_key = norm_grad(*centre(head_part(i, h, 1)), grad_khat)
        bt[0, sums(1, h), image_rows(i)] = grad_key.T.astype(BF16)
        grad_query = norm_grad(*centre(head_part(i, h, 0)), grad_qhat)
        bt[0, sums(2, h), image_rows(i)] = grad_query.T.astype(BF16)

    def gathered(r):
        return rows[r // NZ, :, :, :, columns(r)].reshape(2 * PATCH, PAIR)

    def project(r):
        base = target(r) * PAIR

        @pl.loop(0, PAIR // HD)
        def _(k):
            here = pl.ds(pl.multiple_of(k * HD, HD), HD)
            wpart[here, :] = wq[pl.ds(pl.multiple_of(base + k * HD, HD), HD)].reshape(HD, 6 * HD)

        proj[...] += dot(gathered(r), wpart[...], ((1,), (0,)))

    def project_back(r):
        @pl.loop(0, PAIR // HD)
        def _(k):
            here = pl.ds(pl.multiple_of(k * HD, HD), HD)
            there = pl.ds(pl.multiple_of((k % 3) * HD, HD), HD)
            wpart[here, pl.ds(0, 2 * HD)] = wo[target(r), k // 3, there].reshape(HD, 2 * HD)

        gctx[...] += dot(gathered(r), wpart[:, pl.ds(0, 2 * HD)], ((1,), (0,)))

    weights_across().start()
    send_weights(0)

    @pl.loop(0, ROUNDS + 4)
    def _(it):
        @pl.when(it < ROUNDS)
        def _():
            move(it, 0, x, yl, pair).start()
            move(it, 1, x, yl, right).start()
            move(it, 2, x, yl, left).start()

        for m, when in ((1, 2), (2, 3), (3, 5), (4, 7), (5, 8), (6, 11)):

            @pl.when(it == when)
            def _(m=m):
                send_weights(m)

        @pl.when((it >= 1) & (it < ROUNDS + 1))
        def _():
            r = it - 1
            landed(r, 0, x, 1 - yl)
            move(r, 3, x, 1 - yl, right).start()
            move(r, 4, x, 1 - yl, left).start()
            landed(r, 1, left_x, yl)
            landed(r, 2, right_x, yl)
            onward = place(z, yh, jnp.where(core == 0, right_x, left_x), yl, core)
            move(r, 5, jnp.where(core == 0, left_x, right_x), yl, onward).start()

        @pl.when((it >= 2) & (it < ROUNDS + 2))
        def _():
            r = it - 2
            landed(r, 5, far_x, yl)
            move(r, 6, far_x, yl, pair).start()

        @pl.when((it >= 3) & (it < ROUNDS + 3))
        def _():
            r = it - 3
            landed(r, 3, left_x, 1 - yl)
            landed(r, 4, right_x, 1 - yl)
            landed(r, 6, far_x, 1 - yl)
            swap(r, core).start()

        @pl.when(it == 4)
        def _():
            loads[3].wait()

        @pl.when(it == 12)
        def _():
            weights_landed(6)

        @pl.when((it >= 4) & (it < NZ + 4))
        def _():
            r = it - 4
            swap(r, 1 - core).wait_recv()
            lend(r).start()
            project(r)

        @pl.when(it >= NZ + 4)
        def _():
            r = it - 4
            swap(r, 1 - core).wait_recv()
            project_back(r)

            @pl.when(it < NZ + 8)
            def _():
                forward(it - NZ - 4)

    @pl.loop(0, NZ)
    def _(r):
        lend(r).wait_recv()
        share(r, core).start()

    @pl.loop(0, 4)
    def _(n):
        backward(n)

    @pl.loop(0, 4)
    def _(n):
        hand_over(1, n).start()

    @pl.loop(0, 4)
    def _(n):
        hand_over(2, n).start()

    @pl.loop(NZ, ROUNDS)
    def _(r):
        lend(r).start()

    @pl.loop(0, NZ)
    def _(r):
        share(r, 1 - core).wait_recv()


    def term(g, to_z):
        a = g // 3
        own_cols = pl.ds(pl.multiple_of(to_z * PAIR + yh * SPAN, SPAN), SPAN)
        other_cols = pl.ds(pl.multiple_of(to_z * SPAN, SPAN), SPAN)
        here = pl.ds(pl.multiple_of(g * 2 * HD, 2 * HD), 2 * HD)
        own = rows[a, :, :, :, own_cols].reshape(2 * PATCH, SPAN)
        other = extra[a, :, :, :, other_cols].reshape(2 * PATCH, SPAN)
        return dot(bt[0, here, :], own, ((1,), (0,))) + dot(bt[1, here, :], other, ((1,), (0,)))

    def pass_on(side, s, g, h):
        source = first.at[sums(g, h)] if s == 0 else run.at[side, s - 1, sums(g, h)]
        return remote(
            source, run.at[side, s, sums(g, h)],
            r_send.at[side, s, g * 2 + h], r_recv.at[side, s, g * 2 + h], sides[side],
        )

    def finish(g):
        total = term(g, z)
        for h in range(2):
            part = total[h * HD : (h + 1) * HD]
            for side in range(2):
                pass_on(side, 3, g, h).wait_recv()
                part = part + run[side, 3, sums(g, h)].astype(F32)
            done = part.T.astype(BF16)

            @pl.when(g < 3)
            def _():
                oq_ref[:, pl.ds(pl.multiple_of((h * 3 + 2 - g) * HD, HD), HD)] = done

            @pl.when(g == 3)
            def _():
                oc_ref[:, h * HD : (h + 1) * HD] = done

    @pl.loop(0, 4)
    def _(g):
        @pl.when(g == 3)
        def _():
            @pl.loop(NZ, ROUNDS)
            def _(r):
                share(r, 1 - core).wait_recv()

        @pl.loop(0, 4)
        def _(n):
            hand_over(g, n).wait_recv()

        start = term(g, (z + 4) % NZ)
        for h in range(2):
            first[sums(g, h)] = start[h * HD : (h + 1) * HD].astype(BF16)
            pass_on(h, 0, g, h).start()
        for s in range(1, 4):
            for side in range(2):
                part = term(g, (z + (4 - s if side == 0 else 4 + s)) % NZ)
                for h in (0, 1) if (s > 1 or side == 1) else (1, 0):
                    piece = part[h * HD : (h + 1) * HD]
                    if s > 1 or h == side:
                        pass_on(side, s - 1, g, h).wait_recv()
                        piece = piece + run[side, s - 1, sums(g, h)].astype(F32)
                    run[side, s - 1, sums(g, h)] = piece.astype(BF16)
                    pass_on(side, s, g, h).start()
            if s == 1:

                @pl.when(g > 0)
                def _():
                    finish(g - 1)

        @pl.when(g == 1)
        def _():
            @pl.loop(NZ, ROUNDS)
            def _(r):
                lend(r).wait_recv()
                share(r, core).start()

    finish(3)


    weights_across().wait_send()
    for side in range(2):
        for m in range(7):
            weights(side, m).wait_send()

    @pl.loop(0, ROUNDS)
    def _(r):
        for slot in range(7):
            move(r, slot, x, yl, pair).wait_send()
        swap(r, core).wait_send()
        lend(r).wait_send()
        share(r, core).wait_send()

    @pl.loop(0, 4)
    def _(g):
        for n in range(4):
            hand_over(g, n).wait_send()
        for side in range(2):
            for s in range(4):
                for h in range(2):
                    if s > 0 or h == side:
                        pass_on(side, s, g, h).wait_send()


def body(tokens, w_qkv, w_out, grad_out):
    dma = pltpu.SemaphoreType.DMA
    vmem = pltpu.VMEM
    grad_qkv, grad_wo = pl.pallas_call(
        kernel,
        out_shape=(
            jax.ShapeDtypeStruct((SPAN, 6 * HD), BF16),
            jax.ShapeDtypeStruct((SPAN, 2 * HD), BF16),
        ),
        in_specs=[pl.BlockSpec(memory_space=pl.ANY)] * 4,
        out_specs=(pl.BlockSpec(memory_space=vmem), pl.BlockSpec(memory_space=vmem)),
        scratch_shapes=[
            vmem((2, 8, 2, BLOCK, WIDTH), BF16),
            vmem((2, 8, 2, BLOCK, WIDTH // 2), BF16),
            vmem((WIDTH, 2, 3 * HD), BF16),
            vmem((NZ, 2, SPAN, 2, HD), BF16),
            vmem((PAIR, 6 * HD), BF16),
            vmem((2 * PATCH, 6 * HD), F32),
            vmem((2 * PATCH, 2 * HD), F32),
            vmem((4, 2, PATCH, HD), BF16),
            vmem((4, PATCH, PATCH), F32),
            vmem((2, 8 * HD, 2 * PATCH), BF16),
            vmem((2, 4, 8 * HD, SPAN), BF16),
            vmem((8 * HD, SPAN), BF16),
            dma((4,)),
            dma((ROUNDS, 10)), dma((ROUNDS, 10)),
            dma((2, 7)), dma((2, 7)),
            dma((1,)), dma((1,)),
            dma((4, 4)), dma((4, 4)),
            dma((2, 4, 8)), dma((2, 4, 8)),
        ],
        compiler_params=pltpu.CompilerParams(
            collective_id=0, has_side_effects=True, vmem_limit_bytes=60 << 20
        ),
    )(tokens, w_qkv, w_out, grad_out)
    return grad_qkv.reshape(SPAN, 2, 3 * HD), grad_wo.reshape(SPAN, 2, HD)


def solution(mesh):
    return jax.shard_map(
        body,
        mesh=mesh,
        in_specs=(
            P(("dp", "mp"), None),
            P(None, "mp", None),
            P("dp", "mp", None),
            P(("dp", "mp"), None),
        ),
        out_specs=(P("dp", "mp", None), P("dp", "mp", None)),
        check_vma=False,
    )
```

```python
import jax
import jax.numpy as jnp
from jax import lax
from jax.experimental import pallas as pl
from jax.experimental.pallas import tpu as pltpu
from jax.sharding import PartitionSpec as P

MESH = pl.DeviceIdType.MESH
F32 = jnp.float32
BF16 = jnp.bfloat16

NX, NZ = 4, 8
BLOCK = 32
PATCH = 256
WIDTH = 6144
SPAN = 384
PAIR = 2 * SPAN
ROUNDS = 2 * NZ
HD = 128
EPS = 1e-06
FACTOR = HD ** (-0.5)


def dot(a, b, dims):
    return lax.dot_general(a, b, (dims, ((), ())), preferred_element_type=F32)


def centre(values):
    centred = values - jnp.mean(values, axis=-1, keepdims=True)
    spread = jnp.mean(centred * centred, axis=-1, keepdims=True)
    return centred, lax.rsqrt(spread + EPS)


def norm_grad(centred, scale, grad):
    slope = jnp.mean(grad * centred, axis=-1, keepdims=True) * (scale * scale * scale)
    inner = grad * scale - centred * slope
    return inner - jnp.mean(inner, axis=-1, keepdims=True)


def kernel(
    tok_ref, wq_ref, wo_ref, go_ref,
    oq_ref, oc_ref,
    rows, extra, wq, wo, wpart, proj, gctx, hats, chances, bt, run, first,
    local, g_send, g_recv, w_send, w_recv, y_send, y_recv, b_send, b_recv, r_send, r_recv,
):
    dp, mp = lax.axis_index("dp"), lax.axis_index("mp")
    z, yh = dp // 2, dp % 2
    x, yl, core = mp // 4, (mp // 2) % 2, mp % 2

    def place(z_, yh_, x_, yl_, core_):
        return (z_ * 2 + yh_, x_ * 4 + yl_ * 2 + core_)

    right_x, left_x, far_x = (x + 1) % NX, (x + 3) % NX, (x + 2) % NX
    pair = place(z, yh, x, 1 - yl, core)
    right = place(z, yh, right_x, yl, core)
    left = place(z, yh, left_x, yl, core)
    sibling = place(z, yh, x, yl, 1 - core)
    outer = place(z, 1 - yh, x, 1 - yl, core)
    across = place(z, 1 - yh, x, yl, core)
    up = place((z + 1) % NZ, yh, x, yl, core)
    down = place((z + 7) % NZ, yh, x, yl, core)
    sides = (up, down)

    def remote(src, dst, send, recv, to):
        return pltpu.make_async_remote_copy(
            src_ref=src, dst_ref=dst, send_sem=send, recv_sem=recv, device_id=to, device_id_type=MESH
        )

    barrier = pltpu.get_barrier_semaphore()
    for to in (pair, right, left, sibling, outer, across, up, down):
        pl.semaphore_signal(barrier, inc=1, device_id=to, device_id_type=MESH)

    mine = x * 2 + yl
    loads = (
        pltpu.make_async_copy(tok_ref, rows.at[0, mine, core], local.at[0]),
        pltpu.make_async_copy(go_ref, rows.at[1, mine, core], local.at[1]),
        pltpu.make_async_copy(wo_ref, wo.at[z, yh], local.at[2]),
        pltpu.make_async_copy(wq_ref, wq, local.at[3]),
    )
    for load in loads:
        load.start()
    proj[...] = jnp.zeros_like(proj)
    gctx[...] = jnp.zeros_like(gctx)
    for load in loads[:3]:
        load.wait()
    pl.semaphore_wait(barrier, 8)


    def target(r):
        j = r % NZ
        step = NZ // 2 - (j + 1) // 2
        return (z + jnp.where(j % 2 == 1, step, NZ - step)) % NZ

    def columns(r):
        return pl.ds(pl.multiple_of(target(r) * PAIR, PAIR), PAIR)

    def block(r, bx, by):
        return rows.at[r // NZ, bx * 2 + by, core, :, columns(r)]

    def move(r, slot, bx, by, to):
        part = block(r, bx, by)
        return remote(part, part, g_send.at[r, slot], g_recv.at[r, slot], to)

    def landed(r, slot, bx, by):
        move(r, slot, bx, by, pair).wait_recv()

    def swap(r, lane):
        part = rows.at[r // NZ, :, lane, :, columns(r)]
        return remote(part, part, g_send.at[r, 7], g_recv.at[r, 7], sibling)

    def lend(r):
        cols = pl.ds(pl.multiple_of(target(r) * PAIR + (1 - yh) * SPAN, SPAN), SPAN)
        there = pl.ds(pl.multiple_of(target(r) * SPAN, SPAN), SPAN)
        half = pl.ds(core * 4, 4)
        return remote(
            rows.at[0, half, :, :, cols], extra.at[0, half, :, :, there],
            g_send.at[r, 8], g_recv.at[r, 8], outer,
        )

    def share(r, owner):
        there = pl.ds(pl.multiple_of(target(r) * SPAN, SPAN), SPAN)
        part = extra.at[0, pl.ds(owner * 4, 4), :, :, there]
        return remote(part, part, g_send.at[r, 9], g_recv.at[r, 9], sibling)

    def quarter(r, bx):
        there = pl.ds(pl.multiple_of(target(r) * SPAN, SPAN), SPAN)
        return extra.at[1, pl.ds(bx * 2, 2), core, :, there]

    def give(r):
        cols = pl.ds(pl.multiple_of(target(r) * PAIR + (1 - yh) * SPAN, SPAN), SPAN)
        mine = rows.at[1, pl.ds(x * 2, 2), core, :, cols]
        return remote(mine, quarter(r, x), g_send.at[r, 8], g_recv.at[r, 8], outer)

    def pass_quarter(r, slot, bx, to):
        part = quarter(r, bx)
        return remote(part, part, g_send.at[r, slot], g_recv.at[r, slot], to)

    def swap_quarters(r, lane):
        there = pl.ds(pl.multiple_of(target(r) * SPAN, SPAN), SPAN)
        part = extra.at[1, :, lane, :, there]
        return remote(part, part, g_send.at[r, 9], g_recv.at[r, 9], sibling)


    def weights(side, m):
        hop = m // 2
        from_z = (z + (NZ - hop if side == 0 else hop)) % NZ
        own = (m % 2 == 0) if (m < 6 or side == 0) else False
        part = wo.at[from_z, yh if own else 1 - yh]
        return remote(part, part, w_send.at[side, m], w_recv.at[side, m], sides[side])

    def weights_landed(m):
        for side in range(2):
            weights(side, m).wait_recv()

    def weights_across():
        part = wo.at[z, yh]
        return remote(part, part, y_send.at[0], y_recv.at[0], across)

    def send_weights(m):
        if m == 1:
            weights_across().wait_recv()
        if m >= 2:
            weights_landed(m - 2)
        if m == 6:
            weights_landed(5)
        for side in range(2):
            weights(side, m).start()


    def image_rows(i):
        return pl.ds(pl.multiple_of(i * PATCH, PATCH), PATCH)

    def head_part(i, h, part):
        return proj[image_rows(i), pl.ds(pl.multiple_of((h * 3 + part) * HD, HD), HD)]

    def sums(g, h):
        return pl.ds(pl.multiple_of((g * 2 + h) * HD, HD), HD)

    def hand_over(g, n):
        i, h = n // 2, n % 2
        return remote(
            bt.at[0, sums(g, h), image_rows(i)], bt.at[1, sums(g, h), image_rows(i)],
            b_send.at[g, n], b_recv.at[g, n], across,
        )

    def forward(n):
        i, h = n // 2, n % 2
        centred_q, scale_q = centre(head_part(i, h, 0))
        centred_k, scale_k = centre(head_part(i, h, 1))
        query_hat = (centred_q * scale_q).astype(BF16)
        key_hat = (centred_k * scale_k).astype(BF16)
        value_hat = head_part(i, h, 2).astype(BF16)
        hats[n, 0] = query_hat
        hats[n, 1] = key_hat
        weight = jnp.exp(dot(query_hat, key_hat, ((1,), (1,))) * FACTOR)
        chance = weight / jnp.sum(weight, axis=-1, keepdims=True)
        chances[n] = chance
        context = dot(chance.astype(BF16), value_hat, ((1,), (0,)))
        bt[0, sums(3, h), image_rows(i)] = context.T.astype(BF16)
        hand_over(3, n).start()

    def backward(n):
        i, h = n // 2, n % 2
        chance = chances[n]
        chance_low = chance.astype(BF16)
        query_hat, key_hat = hats[n, 0], hats[n, 1]
        value_hat = head_part(i, h, 2).astype(BF16)
        grad_context = gctx[image_rows(i), pl.ds(pl.multiple_of(h * HD, HD), HD)].astype(BF16)
        grad_value = dot(chance_low, grad_context, ((0,), (0,)))
        bt[0, sums(0, h), image_rows(i)] = grad_value.T.astype(BF16)
        hand_over(0, n).start()
        grad_chance = dot(grad_context, value_hat, ((1,), (1,)))
        inner = jnp.sum(chance * grad_chance, axis=-1, keepdims=True)
        grad_score = (chance * (grad_chance - inner) * FACTOR).astype(BF16)
        grad_qhat = dot(grad_score, key_hat, ((1,), (0,)))
        grad_khat = dot(grad_score, query_hat, ((0,), (0,)))
        grad_key = norm_grad(*centre(head_part(i, h, 1)), grad_khat)
        bt[0, sums(1, h), image_rows(i)] = grad_key.T.astype(BF16)
        grad_query = norm_grad(*centre(head_part(i, h, 0)), grad_qhat)
        bt[0, sums(2, h), image_rows(i)] = grad_query.T.astype(BF16)

    def gathered(r):
        return rows[r // NZ, :, :, :, columns(r)].reshape(2 * PATCH, PAIR)

    def project(r):
        base = target(r) * PAIR

        @pl.loop(0, PAIR // HD)
        def _(k):
            here = pl.ds(pl.multiple_of(k * HD, HD), HD)
            wpart[here, :] = wq[pl.ds(pl.multiple_of(base + k * HD, HD), HD)].reshape(HD, 6 * HD)

        proj[...] += dot(gathered(r), wpart[...], ((1,), (0,)))

    def project_back(r):
        @pl.loop(0, PAIR // HD)
        def _(k):
            here = pl.ds(pl.multiple_of(k * HD, HD), HD)
            there = pl.ds(pl.multiple_of((k % 3) * HD, HD), HD)
            wpart[here, pl.ds(0, 2 * HD)] = wo[target(r), k // 3, there].reshape(HD, 2 * HD)

        gctx[...] += dot(gathered(r), wpart[:, pl.ds(0, 2 * HD)], ((1,), (0,)))


    def term(g, to_z):
        a = g // 3
        own_cols = pl.ds(pl.multiple_of(to_z * PAIR + yh * SPAN, SPAN), SPAN)
        other_cols = pl.ds(pl.multiple_of(to_z * SPAN, SPAN), SPAN)
        here = pl.ds(pl.multiple_of(g * 2 * HD, 2 * HD), 2 * HD)
        own = rows[a, :, :, :, own_cols].reshape(2 * PATCH, SPAN)
        other = extra[a, :, :, :, other_cols].reshape(2 * PATCH, SPAN)
        return dot(bt[0, here, :], own, ((1,), (0,))) + dot(bt[1, here, :], other, ((1,), (0,)))

    def chain(side, s, g, h):
        dp_to = ((z + jnp.where(side == 0, 1, 7)) % NZ) * 2 + yh
        return remote(
            run.at[side, s - 1, sums(g, h)], run.at[side, s, sums(g, h)],
            r_send.at[side, s, g * 2 + h], r_recv.at[side, s, g * 2 + h], (dp_to, mp),
        )

    def chain_start(side, g, h):
        return remote(
            first.at[sums(g, h)], run.at[side, 0, sums(g, h)],
            r_send.at[side, 0, g * 2 + h], r_recv.at[side, 0, g * 2 + h], sides[side],
        )

    def chain_landed(side, s, g, h):
        part = run.at[side, s, sums(g, h)]
        remote(
            part, part, r_send.at[side, s, g * 2 + h], r_recv.at[side, s, g * 2 + h], up
        ).wait_recv()

    def begin(g):
        part = term(g, (z + 4) % NZ)
        for h in range(2):
            first[sums(g, h)] = part[h * HD : (h + 1) * HD].astype(BF16)
            chain_start(h, g, h).start()

    def advance(g, side, s):
        part = term(g, (z + jnp.where(side == 0, 4 - s, 4 + s)) % NZ)
        for h in range(2):
            piece = part[h * HD : (h + 1) * HD]
            arrives = (s > 1) | (side == h)

            @pl.when(arrives)
            def _():
                chain_landed(side, s - 1, g, h)
                here = run[side, s - 1, sums(g, h)].astype(F32)
                run[side, s - 1, sums(g, h)] = (piece + here).astype(BF16)

            @pl.when(jnp.logical_not(arrives))
            def _():
                run[side, s - 1, sums(g, h)] = piece.astype(BF16)

            chain(side, s, g, h).start()

    def finish(g):
        total = term(g, z)
        for h in range(2):
            part = total[h * HD : (h + 1) * HD]
            for side in range(2):
                chain_landed(side, 3, g, h)
                part = part + run[side, 3, sums(g, h)].astype(F32)
            done = part.T.astype(BF16)

            @pl.when(g < 3)
            def _():
                oq_ref[:, pl.ds(pl.multiple_of((h * 3 + 2 - g) * HD, HD), HD)] = done

            @pl.when(g == 3)
            def _():
                oc_ref[:, h * HD : (h + 1) * HD] = done


    def stage(it, lag, least=0, most=ROUNDS):
        return pl.when((it - lag >= least) & (it - lag < most))

    weights_across().start()
    send_weights(0)

    @pl.loop(0, ROUNDS + 12)
    def _(it):
        @stage(it, 0)
        def _():
            move(it, 0, x, yl, pair).start()
            move(it, 1, x, yl, right).start()
            move(it, 2, x, yl, left).start()

        for m, when in ((1, 2), (2, 4), (3, 5), (4, 7), (5, 9), (6, 11)):

            @pl.when(it == when)
            def _(m=m):
                send_weights(m)

        @stage(it, 6)
        def _():
            r = it - 6
            landed(r, 3, left_x, 1 - yl)
            landed(r, 4, right_x, 1 - yl)
            landed(r, 6, far_x, 1 - yl)
            swap(r, core).start()

        @stage(it, 4)
        def _():
            r = it - 4
            landed(r, 5, far_x, yl)
            move(r, 6, far_x, yl, pair).start()

        @stage(it, 2)
        def _():
            r = it - 2
            landed(r, 0, x, 1 - yl)
            move(r, 3, x, 1 - yl, right).start()
            move(r, 4, x, 1 - yl, left).start()
            landed(r, 1, left_x, yl)
            landed(r, 2, right_x, yl)
            onward = place(z, yh, jnp.where(core == 0, right_x, left_x), yl, core)
            move(r, 5, jnp.where(core == 0, left_x, right_x), yl, onward).start()

        @stage(it, 3, NZ)
        def _():
            give(it - 3).start()

        @stage(it, 5, NZ)
        def _():
            r = it - 5
            give(r).wait_recv()
            pass_quarter(r, 10, x, right).start()
            pass_quarter(r, 11, x, left).start()

        @stage(it, 7, NZ)
        def _():
            r = it - 7
            pass_quarter(r, 10, left_x, right).wait_recv()
            pass_quarter(r, 11, right_x, left).wait_recv()
            onward = place(z, yh, jnp.where(core == 0, right_x, left_x), yl, core)
            pass_quarter(r, 12, jnp.where(core == 0, left_x, right_x), onward).start()

        @stage(it, 9, NZ)
        def _():
            r = it - 9
            pass_quarter(r, 12, far_x, right).wait_recv()
            swap_quarters(r, core).start()

        @pl.when((it >= 8) & (it < 24) & (it % 2 == 0))
        def _():
            lend((it - 8) // 2).start()

        @pl.when((it >= 11) & (it < 27) & (it % 2 == 1))
        def _():
            r = (it - 11) // 2
            lend(r).wait_recv()
            share(r, core).start()

        @pl.when(it == 7)
        def _():
            loads[3].wait()

        @pl.when(it == 15)
        def _():
            weights_landed(6)

        @stage(it, 7)
        def _():
            swap(it - 7, 1 - core).wait_recv()

        @stage(it, 7, 0, NZ)
        def _():
            project(it - 7)

        @stage(it, 7, NZ)
        def _():
            project_back(it - 7)

        @stage(it, 15, 0, 4)
        def _():
            forward(it - 15)

        @stage(it, 23, 0, 4)
        def _():
            backward(it - 23)

        @pl.when(it == 20)
        def _():
            for n in range(4):
                hand_over(3, n).wait_recv()

        @stage(it, 12, NZ)
        def _():
            r = it - 12
            j = r - NZ
            swap_quarters(r, 1 - core).wait_recv()

            @pl.when(j == 0)
            def _():
                begin(3)

            @pl.when((j > 0) & (j < 7))
            def _():
                advance(3, 1 - j % 2, (j + 1) // 2)

    @pl.loop(0, 4)
    def _(n):
        hand_over(1, n).start()

    @pl.loop(0, 4)
    def _(n):
        hand_over(2, n).start()

    @pl.loop(0, NZ)
    def _(r):
        share(r, 1 - core).wait_recv()

    def pick(t, table):
        return sum(jnp.where(t == i, v, 0) for i, v in enumerate(table) if v)

    plan = (
        (0, 0), (0, 1), (1, 0), (0, 2), (1, 1), (0, 3), (3, 4), (1, 2), (2, 0), (0, 4),
        (1, 3), (2, 1), (1, 4), (2, 2), (2, 3), (2, 4),
    )

    @pl.loop(0, len(plan))
    def _(t):
        g = pick(t, [g for g, _ in plan])
        s = pick(t, [s for _, s in plan])

        @pl.when(s == 0)
        def _():
            for n in range(4):
                hand_over(g, n).wait_recv()
            begin(g)

        @pl.when((s > 0) & (s < 4))
        def _():
            @pl.loop(0, 2)
            def _(side):
                advance(g, side, s)

        @pl.when(s == 4)
        def _():
            finish(g)


    weights_across().wait_send()
    for side in range(2):
        for m in range(7):
            weights(side, m).wait_send()

    @pl.loop(0, ROUNDS)
    def _(r):
        for slot in range(7):
            move(r, slot, x, yl, pair).wait_send()
        swap(r, core).wait_send()

    @pl.loop(0, NZ)
    def _(r):
        lend(r).wait_send()
        share(r, core).wait_send()

    @pl.loop(NZ, ROUNDS)
    def _(r):
        give(r).wait_send()
        for slot in range(10, 13):
            pass_quarter(r, slot, x, right).wait_send()
        swap_quarters(r, core).wait_send()

    @pl.loop(0, 4)
    def _(g):
        for n in range(4):
            hand_over(g, n).wait_send()
        for side in range(2):
            chain_start(side, g, side).wait_send()
            for s in range(1, 4):
                for h in range(2):
                    chain(side, s, g, h).wait_send()


def body(tokens, w_qkv, w_out, grad_out):
    dma = pltpu.SemaphoreType.DMA
    vmem = pltpu.VMEM
    grad_qkv, grad_wo = pl.pallas_call(
        kernel,
        out_shape=(
            jax.ShapeDtypeStruct((SPAN, 6 * HD), BF16),
            jax.ShapeDtypeStruct((SPAN, 2 * HD), BF16),
        ),
        in_specs=[pl.BlockSpec(memory_space=pl.ANY)] * 4,
        out_specs=(pl.BlockSpec(memory_space=vmem), pl.BlockSpec(memory_space=vmem)),
        scratch_shapes=[
            vmem((2, 8, 2, BLOCK, WIDTH), BF16),
            vmem((2, 8, 2, BLOCK, WIDTH // 2), BF16),
            vmem((WIDTH, 2, 3 * HD), BF16),
            vmem((NZ, 2, SPAN, 2, HD), BF16),
            vmem((PAIR, 6 * HD), BF16),
            vmem((2 * PATCH, 6 * HD), F32),
            vmem((2 * PATCH, 2 * HD), F32),
            vmem((4, 2, PATCH, HD), BF16),
            vmem((4, PATCH, PATCH), F32),
            vmem((2, 8 * HD, 2 * PATCH), BF16),
            vmem((2, 4, 8 * HD, SPAN), BF16),
            vmem((8 * HD, SPAN), BF16),
            dma((4,)),
            dma((ROUNDS, 13)), dma((ROUNDS, 13)),
            dma((2, 7)), dma((2, 7)),
            dma((1,)), dma((1,)),
            dma((4, 4)), dma((4, 4)),
            dma((2, 4, 8)), dma((2, 4, 8)),
        ],
        compiler_params=pltpu.CompilerParams(
            collective_id=0, has_side_effects=True, vmem_limit_bytes=60 << 20
        ),
    )(tokens, w_qkv, w_out, grad_out)
    return grad_qkv.reshape(SPAN, 2, 3 * HD), grad_wo.reshape(SPAN, 2, HD)


def solution(mesh):
    return jax.shard_map(
        body,
        mesh=mesh,
        in_specs=(
            P(("dp", "mp"), None),
            P(None, "mp", None),
            P("dp", "mp", None),
            P(("dp", "mp"), None),
        ),
        out_specs=(P("dp", "mp", None), P("dp", "mp", None)),
        check_vma=False,
    )
```

```python
import jax
import jax.numpy as jnp
from jax import lax
from jax.experimental import pallas as pl
from jax.experimental.pallas import tpu as pltpu
from jax.sharding import PartitionSpec as P

MESH = pl.DeviceIdType.MESH
F32 = jnp.float32
BF16 = jnp.bfloat16

NX, NZ = 4, 8
BLOCK = 32
PATCH = 256
WIDTH = 6144
SPAN = 384
PAIR = 2 * SPAN
ROUNDS = 2 * NZ
HD = 128
EPS = 1e-06
FACTOR = HD ** (-0.5)


def dot(a, b, dims):
    return lax.dot_general(a, b, (dims, ((), ())), preferred_element_type=F32)


def centre(values):
    centred = values - jnp.mean(values, axis=-1, keepdims=True)
    spread = jnp.mean(centred * centred, axis=-1, keepdims=True)
    return centred, lax.rsqrt(spread + EPS)


def norm_grad(centred, scale, grad):
    slope = jnp.mean(grad * centred, axis=-1, keepdims=True) * (scale * scale * scale)
    inner = grad * scale - centred * slope
    return inner - jnp.mean(inner, axis=-1, keepdims=True)


def kernel(
    tok_ref, wq_ref, wo_ref, go_ref,
    oq_ref, oc_ref,
    rows, extra, wq, wo, wpart, proj, gctx, hats, chances, bt, run, first,
    local, sent, g_recv, w_recv, y_recv, b_recv, r_recv,
):
    dp, mp = lax.axis_index("dp"), lax.axis_index("mp")
    z, yh = dp // 2, dp % 2
    x, yl, core = mp // 4, (mp // 2) % 2, mp % 2

    def place(z_, yh_, x_, yl_, core_):
        return (z_ * 2 + yh_, x_ * 4 + yl_ * 2 + core_)

    right_x, left_x, far_x = (x + 1) % NX, (x + 3) % NX, (x + 2) % NX
    pair = place(z, yh, x, 1 - yl, core)
    right = place(z, yh, right_x, yl, core)
    left = place(z, yh, left_x, yl, core)
    sibling = place(z, yh, x, yl, 1 - core)
    outer = place(z, 1 - yh, x, 1 - yl, core)
    across = place(z, 1 - yh, x, yl, core)
    up = place((z + 1) % NZ, yh, x, yl, core)
    down = place((z + 7) % NZ, yh, x, yl, core)
    sides = (up, down)

    def remote(src, dst, send, recv, to):
        return pltpu.make_async_remote_copy(
            src_ref=src, dst_ref=dst, send_sem=send, recv_sem=recv, device_id=to, device_id_type=MESH
        )

    barrier = pltpu.get_barrier_semaphore()
    for to in (pair, right, left, sibling, outer, across, up, down):
        pl.semaphore_signal(barrier, inc=1, device_id=to, device_id_type=MESH)

    mine = x * 2 + yl
    loads = (
        pltpu.make_async_copy(tok_ref, rows.at[0, mine, core], local.at[0]),
        pltpu.make_async_copy(go_ref, rows.at[1, mine, core], local.at[1]),
        pltpu.make_async_copy(wo_ref, wo.at[z, yh], local.at[2]),
        pltpu.make_async_copy(wq_ref, wq, local.at[3]),
    )
    for load in loads:
        load.start()
    proj[...] = jnp.zeros_like(proj)
    gctx[...] = jnp.zeros_like(gctx)
    for load in loads[:3]:
        load.wait()
    pl.semaphore_wait(barrier, 8)


    def target(r):
        j = r % NZ
        step = NZ // 2 - (j + 1) // 2
        return (z + jnp.where(j % 2 == 1, step, NZ - step)) % NZ

    def columns(r):
        return pl.ds(pl.multiple_of(target(r) * PAIR, PAIR), PAIR)

    def block(r, bx, by):
        return rows.at[r // NZ, bx * 2 + by, core, :, columns(r)]

    def move(r, slot, bx, by, to):
        part = block(r, bx, by)
        return remote(part, part, sent.at[0], g_recv.at[r, slot], to)

    def landed(r, slot, bx, by):
        move(r, slot, bx, by, pair).wait_recv()

    def swap(r, lane):
        part = rows.at[r // NZ, :, lane, :, columns(r)]
        return remote(part, part, sent.at[1], g_recv.at[r, 7], sibling)

    def lend(r):
        cols = pl.ds(pl.multiple_of(target(r) * PAIR + (1 - yh) * SPAN, SPAN), SPAN)
        there = pl.ds(pl.multiple_of(target(r) * SPAN, SPAN), SPAN)
        half = pl.ds(core * 4, 4)
        return remote(
            rows.at[0, half, :, :, cols], extra.at[0, half, :, :, there],
            sent.at[2], g_recv.at[r, 8], outer,
        )

    def share(r, owner):
        there = pl.ds(pl.multiple_of(target(r) * SPAN, SPAN), SPAN)
        part = extra.at[0, pl.ds(owner * 4, 4), :, :, there]
        return remote(part, part, sent.at[3], g_recv.at[r, 9], sibling)

    def quarter(r, bx):
        there = pl.ds(pl.multiple_of(target(r) * SPAN, SPAN), SPAN)
        return extra.at[1, pl.ds(bx * 2, 2), core, :, there]

    def give(r):
        cols = pl.ds(pl.multiple_of(target(r) * PAIR + (1 - yh) * SPAN, SPAN), SPAN)
        mine = rows.at[1, pl.ds(x * 2, 2), core, :, cols]
        return remote(mine, quarter(r, x), sent.at[4], g_recv.at[r, 8], outer)

    def pass_quarter(r, slot, bx, to):
        part = quarter(r, bx)
        return remote(part, part, sent.at[5], g_recv.at[r, slot], to)

    def swap_quarters(r, lane):
        there = pl.ds(pl.multiple_of(target(r) * SPAN, SPAN), SPAN)
        part = extra.at[1, :, lane, :, there]
        return remote(part, part, sent.at[6], g_recv.at[r, 9], sibling)


    def weights(side, m):
        hop = m // 2
        from_z = (z + (NZ - hop if side == 0 else hop)) % NZ
        own = (m % 2 == 0) if (m < 6 or side == 0) else False
        part = wo.at[from_z, yh if own else 1 - yh]
        return remote(part, part, sent.at[7], w_recv.at[side, m], sides[side])

    def weights_landed(m):
        for side in range(2):
            weights(side, m).wait_recv()

    def weights_across():
        part = wo.at[z, yh]
        return remote(part, part, sent.at[8], y_recv.at[0], across)

    def send_weights(m):
        if m == 1:
            weights_across().wait_recv()
        if m >= 2:
            weights_landed(m - 2)
        if m == 6:
            weights_landed(5)
        for side in range(2):
            weights(side, m).start()


    def image_rows(i):
        return pl.ds(pl.multiple_of(i * PATCH, PATCH), PATCH)

    def head_part(i, h, part):
        return proj[image_rows(i), pl.ds(pl.multiple_of((h * 3 + part) * HD, HD), HD)]

    def sums(g, h):
        return pl.ds(pl.multiple_of((g * 2 + h) * HD, HD), HD)

    def hand_over(g, n):
        i, h = n // 2, n % 2
        return remote(
            bt.at[0, sums(g, h), image_rows(i)], bt.at[1, sums(g, h), image_rows(i)],
            sent.at[9], b_recv.at[g, n], across,
        )

    def forward(n):
        i, h = n // 2, n % 2
        centred_q, scale_q = centre(head_part(i, h, 0))
        centred_k, scale_k = centre(head_part(i, h, 1))
        query_hat = (centred_q * scale_q).astype(BF16)
        key_hat = (centred_k * scale_k).astype(BF16)
        value_hat = head_part(i, h, 2).astype(BF16)
        hats[n, 0] = query_hat
        hats[n, 1] = key_hat
        weight = jnp.exp(dot(query_hat, key_hat, ((1,), (1,))) * FACTOR)
        chance = weight / jnp.sum(weight, axis=-1, keepdims=True)
        chances[n] = chance
        context = dot(chance.astype(BF16), value_hat, ((1,), (0,)))
        bt[0, sums(3, h), image_rows(i)] = context.T.astype(BF16)
        hand_over(3, n).start()

    def backward(n):
        i, h = n // 2, n % 2
        chance = chances[n]
        chance_low = chance.astype(BF16)
        query_hat, key_hat = hats[n, 0], hats[n, 1]
        value_hat = head_part(i, h, 2).astype(BF16)
        grad_context = gctx[image_rows(i), pl.ds(pl.multiple_of(h * HD, HD), HD)].astype(BF16)
        grad_value = dot(chance_low, grad_context, ((0,), (0,)))
        bt[0, sums(0, h), image_rows(i)] = grad_value.T.astype(BF16)
        hand_over(0, n).start()
        grad_chance = dot(grad_context, value_hat, ((1,), (1,)))
        inner = jnp.sum(chance * grad_chance, axis=-1, keepdims=True)
        grad_score = (chance * (grad_chance - inner) * FACTOR).astype(BF16)
        grad_qhat = dot(grad_score, key_hat, ((1,), (0,)))
        grad_khat = dot(grad_score, query_hat, ((0,), (0,)))
        grad_key = norm_grad(*centre(head_part(i, h, 1)), grad_khat)
        bt[0, sums(1, h), image_rows(i)] = grad_key.T.astype(BF16)
        grad_query = norm_grad(*centre(head_part(i, h, 0)), grad_qhat)
        bt[0, sums(2, h), image_rows(i)] = grad_query.T.astype(BF16)

    def gathered(r):
        return rows[r // NZ, :, :, :, columns(r)].reshape(2 * PATCH, PAIR)

    def project(r):
        base = target(r) * PAIR

        @pl.loop(0, PAIR // HD)
        def _(k):
            here = pl.ds(pl.multiple_of(k * HD, HD), HD)
            wpart[here, :] = wq[pl.ds(pl.multiple_of(base + k * HD, HD), HD)].reshape(HD, 6 * HD)

        proj[...] += dot(gathered(r), wpart[...], ((1,), (0,)))

    def project_back(r):
        @pl.loop(0, PAIR // HD)
        def _(k):
            here = pl.ds(pl.multiple_of(k * HD, HD), HD)
            there = pl.ds(pl.multiple_of((k % 3) * HD, HD), HD)
            wpart[here, pl.ds(0, 2 * HD)] = wo[target(r), k // 3, there].reshape(HD, 2 * HD)

        gctx[...] += dot(gathered(r), wpart[:, pl.ds(0, 2 * HD)], ((1,), (0,)))


    def term(g, to_z):
        a = g // 3
        own_cols = pl.ds(pl.multiple_of(to_z * PAIR + yh * SPAN, SPAN), SPAN)
        other_cols = pl.ds(pl.multiple_of(to_z * SPAN, SPAN), SPAN)
        here = pl.ds(pl.multiple_of(g * 2 * HD, 2 * HD), 2 * HD)
        own = rows[a, :, :, :, own_cols].reshape(2 * PATCH, SPAN)
        other = extra[a, :, :, :, other_cols].reshape(2 * PATCH, SPAN)
        return dot(bt[0, here, :], own, ((1,), (0,))) + dot(bt[1, here, :], other, ((1,), (0,)))

    def chain(side, s, g, h):
        dp_to = ((z + jnp.where(side == 0, 1, 7)) % NZ) * 2 + yh
        return remote(
            run.at[side, s - 1, sums(g, h)], run.at[side, s, sums(g, h)],
            sent.at[10], r_recv.at[side, s, g * 2 + h], (dp_to, mp),
        )

    def chain_start(side, g, h):
        return remote(
            first.at[sums(g, h)], run.at[side, 0, sums(g, h)],
            sent.at[10], r_recv.at[side, 0, g * 2 + h], sides[side],
        )

    def chain_landed(side, s, g, h):
        part = run.at[side, s, sums(g, h)]
        remote(
            part, part, sent.at[10], r_recv.at[side, s, g * 2 + h], up
        ).wait_recv()

    def begin(g):
        part = term(g, (z + 4) % NZ)
        for h in range(2):
            first[sums(g, h)] = part[h * HD : (h + 1) * HD].astype(BF16)
            chain_start(h, g, h).start()

    def advance(g, side, s):
        part = term(g, (z + jnp.where(side == 0, 4 - s, 4 + s)) % NZ)
        for h in range(2):
            piece = part[h * HD : (h + 1) * HD]
            arrives = (s > 1) | (side == h)

            @pl.when(arrives)
            def _():
                chain_landed(side, s - 1, g, h)
                here = run[side, s - 1, sums(g, h)].astype(F32)
                run[side, s - 1, sums(g, h)] = (piece + here).astype(BF16)

            @pl.when(jnp.logical_not(arrives))
            def _():
                run[side, s - 1, sums(g, h)] = piece.astype(BF16)

            chain(side, s, g, h).start()

    def finish(g):
        total = term(g, z)
        for h in range(2):
            part = total[h * HD : (h + 1) * HD]
            for side in range(2):
                chain_landed(side, 3, g, h)
                part = part + run[side, 3, sums(g, h)].astype(F32)
            done = part.T.astype(BF16)

            @pl.when(g < 3)
            def _():
                oq_ref[:, pl.ds(pl.multiple_of((h * 3 + 2 - g) * HD, HD), HD)] = done

            @pl.when(g == 3)
            def _():
                oc_ref[:, h * HD : (h + 1) * HD] = done


    def stage(it, lag, least=0, most=ROUNDS):
        return pl.when((it - lag >= least) & (it - lag < most))

    weights_across().start()
    send_weights(0)

    @pl.loop(0, ROUNDS + 11)
    def _(it):
        @stage(it, 0)
        def _():
            move(it, 0, x, yl, pair).start()
            move(it, 1, x, yl, right).start()
            move(it, 2, x, yl, left).start()

        for m, when in ((1, 2), (2, 4), (3, 5), (4, 7), (5, 9), (6, 11)):

            @pl.when(it == when)
            def _(m=m):
                send_weights(m)

        @stage(it, 6)
        def _():
            r = it - 6
            landed(r, 3, left_x, 1 - yl)
            landed(r, 4, right_x, 1 - yl)
            landed(r, 6, far_x, 1 - yl)
            swap(r, core).start()

        @stage(it, 4)
        def _():
            r = it - 4
            landed(r, 5, far_x, yl)
            move(r, 6, far_x, yl, pair).start()

        @stage(it, 2)
        def _():
            r = it - 2
            landed(r, 0, x, 1 - yl)
            move(r, 3, x, 1 - yl, right).start()
            move(r, 4, x, 1 - yl, left).start()
            landed(r, 1, left_x, yl)
            landed(r, 2, right_x, yl)
            onward = place(z, yh, jnp.where(core == 0, right_x, left_x), yl, core)
            move(r, 5, jnp.where(core == 0, left_x, right_x), yl, onward).start()

        @stage(it, 3, NZ)
        def _():
            give(it - 3).start()

        @stage(it, 5, NZ)
        def _():
            r = it - 5
            give(r).wait_recv()
            pass_quarter(r, 10, x, right).start()
            pass_quarter(r, 11, x, left).start()

        @stage(it, 7, NZ)
        def _():
            r = it - 7
            pass_quarter(r, 10, left_x, right).wait_recv()
            pass_quarter(r, 11, right_x, left).wait_recv()
            onward = place(z, yh, jnp.where(core == 0, right_x, left_x), yl, core)
            pass_quarter(r, 12, jnp.where(core == 0, left_x, right_x), onward).start()

        @stage(it, 9, NZ)
        def _():
            r = it - 9
            pass_quarter(r, 12, far_x, right).wait_recv()
            swap_quarters(r, core).start()

        @pl.when((it >= 8) & (it < 24) & (it % 2 == 0))
        def _():
            lend((it - 8) // 2).start()

        @pl.when((it >= 11) & (it < 27) & (it % 2 == 1))
        def _():
            r = (it - 11) // 2
            lend(r).wait_recv()
            share(r, core).start()

        @pl.when(it == 7)
        def _():
            loads[3].wait()

        @pl.when(it == 15)
        def _():
            weights_landed(6)

        @stage(it, 7)
        def _():
            swap(it - 7, 1 - core).wait_recv()

        @stage(it, 7, 0, NZ)
        def _():
            project(it - 7)

        @stage(it, 7, NZ)
        def _():
            project_back(it - 7)

        @stage(it, 15, 0, 4)
        def _():
            forward(it - 15)

        @stage(it, 23, 0, 4)
        def _():
            backward(it - 23)

        @pl.when(it == 19)
        def _():
            for n in range(4):
                hand_over(3, n).wait_recv()

        @stage(it, 11, NZ)
        def _():
            r = it - 11
            j = r - NZ
            swap_quarters(r, 1 - core).wait_recv()

            @pl.when(j == 0)
            def _():
                begin(3)

            @pl.when((j > 0) & (j < 7))
            def _():
                advance(3, 1 - j % 2, (j + 1) // 2)

    @pl.loop(0, 4)
    def _(n):
        hand_over(1, n).start()

    @pl.loop(0, 4)
    def _(n):
        hand_over(2, n).start()

    @pl.loop(0, NZ)
    def _(r):
        share(r, 1 - core).wait_recv()

    def pick(t, table):
        return sum(jnp.where(t == i, v, 0) for i, v in enumerate(table) if v)

    plan = (
        (0, 0), (0, 1), (1, 0), (0, 2), (1, 1), (0, 3), (3, 4), (1, 2), (2, 0), (0, 4),
        (1, 3), (2, 1), (1, 4), (2, 2), (2, 3), (2, 4),
    )

    @pl.loop(0, len(plan))
    def _(t):
        g = pick(t, [g for g, _ in plan])
        s = pick(t, [s for _, s in plan])

        @pl.when(s == 0)
        def _():
            for n in range(4):
                hand_over(g, n).wait_recv()
            begin(g)

        @pl.when((s > 0) & (s < 4))
        def _():
            @pl.loop(0, 2)
            def _(side):
                advance(g, side, s)

        @pl.when(s == 4)
        def _():
            finish(g)


    gone = (
        rows.at[:, pl.ds(0, 7), core],
        rows.at[:, :, core],
        extra.at[0, pl.ds(0, 4)],
        extra.at[0, pl.ds(0, 4)],
        extra.at[1, pl.ds(0, 2), core],
        extra.at[1, pl.ds(0, 6), core],
        extra.at[1, :, core],
        wo.at[pl.ds(0, 7)],
        wo.at[0, 0],
        bt.at[0],
        run.at[:, :, pl.ds(0, 7 * HD)],
    )
    for kind, part in enumerate(gone):
        remote(part, part, sent.at[kind], y_recv.at[0], up).wait_send()


def split_heads(qkv_ref, out_ref, qkv_heads_ref, out_heads_ref):
    @pl.loop(0, SPAN // HD)
    def _(k):
        here = pl.ds(pl.multiple_of(k * HD, HD), HD)
        qkv_heads_ref[here] = qkv_ref[here].reshape(HD, 2, 3 * HD)
        out_heads_ref[here] = out_ref[here].reshape(HD, 2, HD)


def body(tokens, w_qkv, w_out, grad_out):
    dma = pltpu.SemaphoreType.DMA
    vmem = pltpu.VMEM
    grad_qkv, grad_wo = pl.pallas_call(
        kernel,
        out_shape=(
            jax.ShapeDtypeStruct((SPAN, 6 * HD), BF16),
            jax.ShapeDtypeStruct((SPAN, 2 * HD), BF16),
        ),
        in_specs=[pl.BlockSpec(memory_space=pl.ANY)] * 4,
        out_specs=(pl.BlockSpec(memory_space=vmem), pl.BlockSpec(memory_space=vmem)),
        scratch_shapes=[
            vmem((2, 8, 2, BLOCK, WIDTH), BF16),
            vmem((2, 8, 2, BLOCK, WIDTH // 2), BF16),
            vmem((WIDTH, 2, 3 * HD), BF16),
            vmem((NZ, 2, SPAN, 2, HD), BF16),
            vmem((PAIR, 6 * HD), BF16),
            vmem((2 * PATCH, 6 * HD), F32),
            vmem((2 * PATCH, 2 * HD), F32),
            vmem((4, 2, PATCH, HD), BF16),
            vmem((4, PATCH, PATCH), F32),
            vmem((2, 8 * HD, 2 * PATCH), BF16),
            vmem((2, 4, 8 * HD, SPAN), BF16),
            vmem((8 * HD, SPAN), BF16),
            dma((4,)),
            dma((11,)),
            dma((ROUNDS, 13)),
            dma((2, 7)),
            dma((1,)),
            dma((4, 4)),
            dma((2, 4, 8)),
        ],
        compiler_params=pltpu.CompilerParams(
            collective_id=0, has_side_effects=True, vmem_limit_bytes=60 << 20
        ),
    )(tokens, w_qkv, w_out, grad_out)
    return pl.pallas_call(
        split_heads,
        out_shape=(
            jax.ShapeDtypeStruct((SPAN, 2, 3 * HD), BF16),
            jax.ShapeDtypeStruct((SPAN, 2, HD), BF16),
        ),
        in_specs=[pl.BlockSpec(memory_space=vmem)] * 2,
        out_specs=(pl.BlockSpec(memory_space=vmem), pl.BlockSpec(memory_space=vmem)),
    )(grad_qkv, grad_wo)


def solution(mesh):
    return jax.shard_map(
        body,
        mesh=mesh,
        in_specs=(
            P(("dp", "mp"), None),
            P(None, "mp", None),
            P("dp", "mp", None),
            P(("dp", "mp"), None),
        ),
        out_specs=(P("dp", "mp", None), P("dp", "mp", None)),
        check_vma=False,
    )
```

```python
import jax
import jax.numpy as jnp
from jax import lax
from jax.experimental import pallas as pl
from jax.experimental.pallas import tpu as pltpu
from jax.sharding import PartitionSpec as P

MESH = pl.DeviceIdType.MESH
F32 = jnp.float32
BF16 = jnp.bfloat16

NX, NZ = 4, 8
BLOCK = 32
PATCH = 256
WIDTH = 6144
SPAN = 384
PAIR = 2 * SPAN
ROUNDS = 2 * NZ
ARRIVES = {0: 0, 1: 1, 2: 1, 3: 2, 4: 2, 5: 3, 6: 2, 10: 7, 11: 7, 12: 8}
HD = 128
EPS = 1e-06
FACTOR = HD ** (-0.5)


def dot(a, b, dims):
    return lax.dot_general(a, b, (dims, ((), ())), preferred_element_type=F32)


def centre(values):
    centred = values - jnp.mean(values, axis=-1, keepdims=True)
    spread = jnp.mean(centred * centred, axis=-1, keepdims=True)
    return centred, lax.rsqrt(spread + EPS)


def norm_grad(centred, scale, grad):
    slope = jnp.mean(grad * centred, axis=-1, keepdims=True) * (scale * scale * scale)
    inner = grad * scale - centred * slope
    return inner - jnp.mean(inner, axis=-1, keepdims=True)


def kernel(
    tok_ref, wq_ref, wo_ref, go_ref,
    oq_ref, oc_ref,
    rows, extra, wq, wo, wpart, proj, gctx, hats, chances, bt, run, first,
    local, sent, g_recv, w_recv, y_recv, b_recv, r_recv,
):
    dp, mp = lax.axis_index("dp"), lax.axis_index("mp")
    z, yh = dp // 2, dp % 2
    x, yl, core = mp // 4, (mp // 2) % 2, mp % 2

    def place(z_, yh_, x_, yl_, core_):
        return (z_ * 2 + yh_, x_ * 4 + yl_ * 2 + core_)

    right_x, left_x, far_x = (x + 1) % NX, (x + 3) % NX, (x + 2) % NX
    pair = place(z, yh, x, 1 - yl, core)
    right = place(z, yh, right_x, yl, core)
    left = place(z, yh, left_x, yl, core)
    sibling = place(z, yh, x, yl, 1 - core)
    outer = place(z, 1 - yh, x, 1 - yl, core)
    across = place(z, 1 - yh, x, yl, core)
    up = place((z + 1) % NZ, yh, x, yl, core)
    down = place((z + 7) % NZ, yh, x, yl, core)
    sides = (up, down)

    def remote(src, dst, send, recv, to):
        return pltpu.make_async_remote_copy(
            src_ref=src, dst_ref=dst, send_sem=send, recv_sem=recv, device_id=to, device_id_type=MESH
        )

    barrier = pltpu.get_barrier_semaphore()
    for to in (pair, right, left, sibling, outer, across, up, down):
        pl.semaphore_signal(barrier, inc=1, device_id=to, device_id_type=MESH)

    mine = x * 2 + yl
    loads = (
        pltpu.make_async_copy(tok_ref, rows.at[0, mine, core], local.at[0]),
        pltpu.make_async_copy(go_ref, rows.at[1, mine, core], local.at[1]),
        pltpu.make_async_copy(wo_ref, wo.at[z, yh], local.at[2]),
        pltpu.make_async_copy(wq_ref, wq, local.at[3]),
    )
    for load in loads:
        load.start()
    proj[...] = jnp.zeros_like(proj)
    gctx[...] = jnp.zeros_like(gctx)
    for load in loads[:3]:
        load.wait()
    pl.semaphore_wait(barrier, 8)


    def target(r):
        j = r % NZ
        step = NZ // 2 - (j + 1) // 2
        return (z + jnp.where(j % 2 == 1, step, NZ - step)) % NZ

    def columns(r):
        return pl.ds(pl.multiple_of(target(r) * PAIR, PAIR), PAIR)

    def block(r, bx, by):
        return rows.at[r // NZ, bx * 2 + by, core, :, columns(r)]

    def move(r, slot, bx, by, to):
        part = block(r, bx, by)
        return remote(part, part, sent.at[0], g_recv.at[r, ARRIVES[slot]], to)

    def landed(r, slot, bx, by):
        move(r, slot, bx, by, pair).wait_recv()

    def landed_all(r, slot, count):
        part = rows.at[r // NZ, pl.ds(0, count), core, :, columns(r)]
        remote(part, part, sent.at[0], g_recv.at[r, ARRIVES[slot]], pair).wait_recv()

    def swap(r, lane):
        part = rows.at[r // NZ, :, lane, :, columns(r)]
        return remote(part, part, sent.at[1], g_recv.at[r, 4], sibling)

    def lend(r):
        cols = pl.ds(pl.multiple_of(target(r) * PAIR + (1 - yh) * SPAN, SPAN), SPAN)
        there = pl.ds(pl.multiple_of(target(r) * SPAN, SPAN), SPAN)
        half = pl.ds(core * 4, 4)
        return remote(
            rows.at[0, half, :, :, cols], extra.at[0, half, :, :, there],
            sent.at[2], g_recv.at[r, 5], outer,
        )

    def share(r, owner):
        there = pl.ds(pl.multiple_of(target(r) * SPAN, SPAN), SPAN)
        part = extra.at[0, pl.ds(owner * 4, 4), :, :, there]
        return remote(part, part, sent.at[3], g_recv.at[r, 6], sibling)

    def quarter(r, bx):
        there = pl.ds(pl.multiple_of(target(r) * SPAN, SPAN), SPAN)
        return extra.at[1, pl.ds(bx * 2, 2), core, :, there]

    def give(r):
        cols = pl.ds(pl.multiple_of(target(r) * PAIR + (1 - yh) * SPAN, SPAN), SPAN)
        mine = rows.at[1, pl.ds(x * 2, 2), core, :, cols]
        return remote(mine, quarter(r, x), sent.at[4], g_recv.at[r, 5], outer)

    def pass_quarter(r, slot, bx, to):
        part = quarter(r, bx)
        return remote(part, part, sent.at[5], g_recv.at[r, ARRIVES[slot]], to)

    def swap_quarters(r, lane):
        there = pl.ds(pl.multiple_of(target(r) * SPAN, SPAN), SPAN)
        part = extra.at[1, :, lane, :, there]
        return remote(part, part, sent.at[6], g_recv.at[r, 6], sibling)


    def weights(side, m):
        hop = m // 2
        from_z = (z + (NZ - hop if side == 0 else hop)) % NZ
        own = (m % 2 == 0) if (m < 6 or side == 0) else False
        part = wo.at[from_z, yh if own else 1 - yh]
        return remote(part, part, sent.at[7], w_recv.at[side, m], sides[side])

    def weights_landed(m):
        for side in range(2):
            weights(side, m).wait_recv()

    def weights_across():
        part = wo.at[z, yh]
        return remote(part, part, sent.at[8], y_recv.at[0], across)

    def send_weights(m):
        if m == 1:
            weights_across().wait_recv()
        if m >= 2:
            weights_landed(m - 2)
        if m == 6:
            weights_landed(5)
        for side in range(2):
            weights(side, m).start()


    def image_rows(i):
        return pl.ds(pl.multiple_of(i * PATCH, PATCH), PATCH)

    def head_part(i, h, part):
        return proj[image_rows(i), pl.ds(pl.multiple_of((h * 3 + part) * HD, HD), HD)]

    def sums(g, h):
        return pl.ds(pl.multiple_of((g * 2 + h) * HD, HD), HD)

    def hand_over(g, n):
        i, h = n // 2, n % 2
        return remote(
            bt.at[0, sums(g, h), image_rows(i)], bt.at[1, sums(g, h), image_rows(i)],
            sent.at[9], b_recv.at[g, n], across,
        )

    def forward(n):
        i, h = n // 2, n % 2
        centred_q, scale_q = centre(head_part(i, h, 0))
        centred_k, scale_k = centre(head_part(i, h, 1))
        query_hat = (centred_q * scale_q).astype(BF16)
        key_hat = (centred_k * scale_k).astype(BF16)
        value_hat = head_part(i, h, 2).astype(BF16)
        hats[n, 0] = query_hat
        hats[n, 1] = key_hat
        weight = jnp.exp(dot(query_hat, key_hat, ((1,), (1,))) * FACTOR)
        chance = weight / jnp.sum(weight, axis=-1, keepdims=True)
        chances[n] = chance
        context = dot(chance.astype(BF16), value_hat, ((1,), (0,)))
        bt[0, sums(3, h), image_rows(i)] = context.T.astype(BF16)
        hand_over(3, n).start()

    def backward(n):
        i, h = n // 2, n % 2
        chance = chances[n]
        chance_low = chance.astype(BF16)
        query_hat, key_hat = hats[n, 0], hats[n, 1]
        value_hat = head_part(i, h, 2).astype(BF16)
        grad_context = gctx[image_rows(i), pl.ds(pl.multiple_of(h * HD, HD), HD)].astype(BF16)
        grad_value = dot(chance_low, grad_context, ((0,), (0,)))
        bt[0, sums(0, h), image_rows(i)] = grad_value.T.astype(BF16)
        hand_over(0, n).start()
        grad_chance = dot(grad_context, value_hat, ((1,), (1,)))
        inner = jnp.sum(chance * grad_chance, axis=-1, keepdims=True)
        grad_score = (chance * (grad_chance - inner) * FACTOR).astype(BF16)
        grad_qhat = dot(grad_score, key_hat, ((1,), (0,)))
        grad_khat = dot(grad_score, query_hat, ((0,), (0,)))
        grad_key = norm_grad(*centre(head_part(i, h, 1)), grad_khat)
        bt[0, sums(1, h), image_rows(i)] = grad_key.T.astype(BF16)
        grad_query = norm_grad(*centre(head_part(i, h, 0)), grad_qhat)
        bt[0, sums(2, h), image_rows(i)] = grad_query.T.astype(BF16)

    def gathered(r):
        return rows[r // NZ, :, :, :, columns(r)].reshape(2 * PATCH, PAIR)

    def project(r):
        base = target(r) * PAIR

        @pl.loop(0, PAIR // HD)
        def _(k):
            here = pl.ds(pl.multiple_of(k * HD, HD), HD)
            wpart[here, :] = wq[pl.ds(pl.multiple_of(base + k * HD, HD), HD)].reshape(HD, 6 * HD)

        proj[...] += dot(gathered(r), wpart[...], ((1,), (0,)))

    def project_back(r):
        @pl.loop(0, PAIR // HD)
        def _(k):
            here = pl.ds(pl.multiple_of(k * HD, HD), HD)
            there = pl.ds(pl.multiple_of((k % 3) * HD, HD), HD)
            wpart[here, pl.ds(0, 2 * HD)] = wo[target(r), k // 3, there].reshape(HD, 2 * HD)

        gctx[...] += dot(gathered(r), wpart[:, pl.ds(0, 2 * HD)], ((1,), (0,)))


    def term(g, to_z):
        a = g // 3
        own_cols = pl.ds(pl.multiple_of(to_z * PAIR + yh * SPAN, SPAN), SPAN)
        other_cols = pl.ds(pl.multiple_of(to_z * SPAN, SPAN), SPAN)
        here = pl.ds(pl.multiple_of(g * 2 * HD, 2 * HD), 2 * HD)
        own = rows[a, :, :, :, own_cols].reshape(2 * PATCH, SPAN)
        other = extra[a, :, :, :, other_cols].reshape(2 * PATCH, SPAN)
        return dot(bt[0, here, :], own, ((1,), (0,))) + dot(bt[1, here, :], other, ((1,), (0,)))

    def chain(side, s, g, h):
        dp_to = ((z + jnp.where(side == 0, 1, 7)) % NZ) * 2 + yh
        return remote(
            run.at[side, s - 1, sums(g, h)], run.at[side, s, sums(g, h)],
            sent.at[10], r_recv.at[side, s, g * 2 + h], (dp_to, mp),
        )

    def chain_start(side, g, h):
        return remote(
            first.at[sums(g, h)], run.at[side, 0, sums(g, h)],
            sent.at[10], r_recv.at[side, 0, g * 2 + h], sides[side],
        )

    def chain_landed(side, s, g, h):
        part = run.at[side, s, sums(g, h)]
        remote(
            part, part, sent.at[10], r_recv.at[side, s, g * 2 + h], up
        ).wait_recv()

    def begin(g):
        part = term(g, (z + 4) % NZ)
        for h in range(2):
            first[sums(g, h)] = part[h * HD : (h + 1) * HD].astype(BF16)
            chain_start(h, g, h).start()

    def advance(g, side, s):
        part = term(g, (z + jnp.where(side == 0, 4 - s, 4 + s)) % NZ)
        for h in range(2):
            piece = part[h * HD : (h + 1) * HD]
            arrives = (s > 1) | (side == h)

            @pl.when(arrives)
            def _():
                chain_landed(side, s - 1, g, h)
                here = run[side, s - 1, sums(g, h)].astype(F32)
                run[side, s - 1, sums(g, h)] = (piece + here).astype(BF16)

            @pl.when(jnp.logical_not(arrives))
            def _():
                run[side, s - 1, sums(g, h)] = piece.astype(BF16)

            chain(side, s, g, h).start()

    def finish(g):
        total = term(g, z)
        for h in range(2):
            part = total[h * HD : (h + 1) * HD]
            for side in range(2):
                chain_landed(side, 3, g, h)
                part = part + run[side, 3, sums(g, h)].astype(F32)
            done = part.T.astype(BF16)

            @pl.when(g < 3)
            def _():
                oq_ref[:, pl.ds(pl.multiple_of((h * 3 + 2 - g) * HD, HD), HD)] = done

            @pl.when(g == 3)
            def _():
                oc_ref[:, h * HD : (h + 1) * HD] = done


    def stage(it, lag, least=0, most=ROUNDS):
        return pl.when((it - lag >= least) & (it - lag < most))

    weights_across().start()
    send_weights(0)

    @pl.loop(0, ROUNDS + 11)
    def _(it):
        @stage(it, 0)
        def _():
            move(it, 0, x, yl, pair).start()
            move(it, 1, x, yl, right).start()
            move(it, 2, x, yl, left).start()

        for m, when in ((1, 2), (2, 4), (3, 5), (4, 7), (5, 9), (6, 11)):

            @pl.when(it == when)
            def _(m=m):
                send_weights(m)

        @stage(it, 23, 0, 4)
        def _():
            backward(it - 23)

        @stage(it, 6)
        def _():
            r = it - 6
            landed_all(r, 3, 3)
            swap(r, core).start()

        @stage(it, 4)
        def _():
            r = it - 4
            landed(r, 5, far_x, yl)
            move(r, 6, far_x, yl, pair).start()

        @stage(it, 2)
        def _():
            r = it - 2
            landed(r, 0, x, 1 - yl)
            move(r, 3, x, 1 - yl, right).start()
            move(r, 4, x, 1 - yl, left).start()
            landed_all(r, 1, 2)
            onward = place(z, yh, jnp.where(core == 0, right_x, left_x), yl, core)
            move(r, 5, jnp.where(core == 0, left_x, right_x), yl, onward).start()

        @stage(it, 3, NZ)
        def _():
            give(it - 3).start()

        @stage(it, 5, NZ)
        def _():
            r = it - 5
            give(r).wait_recv()
            pass_quarter(r, 10, x, right).start()
            pass_quarter(r, 11, x, left).start()

        @stage(it, 7, NZ)
        def _():
            r = it - 7
            there = pl.ds(pl.multiple_of(target(r) * SPAN, SPAN), SPAN)
            both = extra.at[1, pl.ds(0, 4), core, :, there]
            remote(both, both, sent.at[5], g_recv.at[r, 7], right).wait_recv()
            onward = place(z, yh, jnp.where(core == 0, right_x, left_x), yl, core)
            pass_quarter(r, 12, jnp.where(core == 0, left_x, right_x), onward).start()

        @stage(it, 9, NZ)
        def _():
            r = it - 9
            pass_quarter(r, 12, far_x, right).wait_recv()
            swap_quarters(r, core).start()

        @pl.when((it >= 8) & (it < 24) & (it % 2 == 0))
        def _():
            lend((it - 8) // 2).start()

        @pl.when((it >= 11) & (it < 27) & (it % 2 == 1))
        def _():
            r = (it - 11) // 2
            lend(r).wait_recv()
            share(r, core).start()

        @pl.when(it == 7)
        def _():
            loads[3].wait()

        @pl.when(it == 15)
        def _():
            weights_landed(6)

        @stage(it, 7)
        def _():
            swap(it - 7, 1 - core).wait_recv()

        @stage(it, 7, 0, NZ)
        def _():
            project(it - 7)

        @stage(it, 7, NZ)
        def _():
            project_back(it - 7)

        @stage(it, 15, 0, 4)
        def _():
            forward(it - 15)

        @pl.when(it == 19)
        def _():
            for n in range(4):
                hand_over(3, n).wait_recv()

        @stage(it, 11, NZ)
        def _():
            r = it - 11
            j = r - NZ
            swap_quarters(r, 1 - core).wait_recv()

            @pl.when(j == 0)
            def _():
                begin(3)

            @pl.when((j > 0) & (j < 7))
            def _():
                advance(3, 1 - j % 2, (j + 1) // 2)

    @pl.loop(0, 4)
    def _(n):
        hand_over(1, n).start()

    @pl.loop(0, 4)
    def _(n):
        hand_over(2, n).start()

    @pl.loop(0, NZ)
    def _(r):
        share(r, 1 - core).wait_recv()

    def pick(t, table):
        return sum(jnp.where(t == i, v, 0) for i, v in enumerate(table) if v)

    plan = (
        (0, 0), (0, 1), (1, 0), (0, 2), (1, 1), (0, 3), (3, 4), (1, 2), (2, 0), (0, 4),
        (1, 3), (2, 1), (1, 4), (2, 2), (2, 3), (2, 4),
    )

    @pl.loop(0, len(plan))
    def _(t):
        g = pick(t, [g for g, _ in plan])
        s = pick(t, [s for _, s in plan])

        @pl.when(s == 0)
        def _():
            for n in range(4):
                hand_over(g, n).wait_recv()
            begin(g)

        @pl.when((s > 0) & (s < 4))
        def _():
            @pl.loop(0, 2)
            def _(side):
                advance(g, side, s)

        @pl.when(s == 4)
        def _():
            finish(g)


    gone = (
        rows.at[:, pl.ds(0, 7), core],
        rows.at[:, :, core],
        extra.at[0, pl.ds(0, 4)],
        extra.at[0, pl.ds(0, 4)],
        extra.at[1, pl.ds(0, 2), core],
        extra.at[1, pl.ds(0, 6), core],
        extra.at[1, :, core],
        wo.at[pl.ds(0, 7)],
        wo.at[0, 0],
        bt.at[0],
        run.at[:, :, pl.ds(0, 7 * HD)],
    )
    for kind, part in enumerate(gone):
        remote(part, part, sent.at[kind], y_recv.at[0], up).wait_send()


def split_heads(qkv_ref, out_ref, qkv_heads_ref, out_heads_ref):
    @pl.loop(0, SPAN // HD)
    def _(k):
        here = pl.ds(pl.multiple_of(k * HD, HD), HD)
        qkv_heads_ref[here] = qkv_ref[here].reshape(HD, 2, 3 * HD)
        out_heads_ref[here] = out_ref[here].reshape(HD, 2, HD)


def body(tokens, w_qkv, w_out, grad_out):
    dma = pltpu.SemaphoreType.DMA
    vmem = pltpu.VMEM
    grad_qkv, grad_wo = pl.pallas_call(
        kernel,
        out_shape=(
            jax.ShapeDtypeStruct((SPAN, 6 * HD), BF16),
            jax.ShapeDtypeStruct((SPAN, 2 * HD), BF16),
        ),
        in_specs=[pl.BlockSpec(memory_space=pl.ANY)] * 4,
        out_specs=(pl.BlockSpec(memory_space=vmem), pl.BlockSpec(memory_space=vmem)),
        scratch_shapes=[
            vmem((2, 8, 2, BLOCK, WIDTH), BF16),
            vmem((2, 8, 2, BLOCK, WIDTH // 2), BF16),
            vmem((WIDTH, 2, 3 * HD), BF16),
            vmem((NZ, 2, SPAN, 2, HD), BF16),
            vmem((PAIR, 6 * HD), BF16),
            vmem((2 * PATCH, 6 * HD), F32),
            vmem((2 * PATCH, 2 * HD), F32),
            vmem((4, 2, PATCH, HD), BF16),
            vmem((4, PATCH, PATCH), F32),
            vmem((2, 8 * HD, 2 * PATCH), BF16),
            vmem((2, 4, 8 * HD, SPAN), BF16),
            vmem((8 * HD, SPAN), BF16),
            dma((4,)),
            dma((11,)),
            dma((ROUNDS, 9)),
            dma((2, 7)),
            dma((1,)),
            dma((4, 4)),
            dma((2, 4, 8)),
        ],
        compiler_params=pltpu.CompilerParams(
            collective_id=0, has_side_effects=True, vmem_limit_bytes=60 << 20
        ),
    )(tokens, w_qkv, w_out, grad_out)
    return pl.pallas_call(
        split_heads,
        out_shape=(
            jax.ShapeDtypeStruct((SPAN, 2, 3 * HD), BF16),
            jax.ShapeDtypeStruct((SPAN, 2, HD), BF16),
        ),
        in_specs=[pl.BlockSpec(memory_space=vmem)] * 2,
        out_specs=(pl.BlockSpec(memory_space=vmem), pl.BlockSpec(memory_space=vmem)),
    )(grad_qkv, grad_wo)


def solution(mesh):
    return jax.shard_map(
        body,
        mesh=mesh,
        in_specs=(
            P(("dp", "mp"), None),
            P(None, "mp", None),
            P("dp", "mp", None),
            P(("dp", "mp"), None),
        ),
        out_specs=(P("dp", "mp", None), P("dp", "mp", None)),
        check_vma=False,
    )
```

```python
import jax
import jax.numpy as jnp
from jax import lax
from jax.experimental import pallas as pl
from jax.experimental.pallas import tpu as pltpu
from jax.sharding import PartitionSpec as P

MESH = pl.DeviceIdType.MESH
F32 = jnp.float32
BF16 = jnp.bfloat16

NX, NZ = 4, 8
BLOCK = 32
PATCH = 256
WIDTH = 6144
SPAN = 384
PAIR = 2 * SPAN
ROUNDS = 2 * NZ
ARRIVES = {0: 0, 1: 1, 2: 1, 3: 2, 4: 2, 5: 3, 6: 2, 10: 7, 11: 7, 12: 8}
HD = 128
EPS = 1e-06
FACTOR = HD ** (-0.5)


def dot(a, b, dims):
    return lax.dot_general(a, b, (dims, ((), ())), preferred_element_type=F32)


def centre(values):
    centred = values - jnp.mean(values, axis=-1, keepdims=True)
    spread = jnp.mean(centred * centred, axis=-1, keepdims=True)
    return centred, lax.rsqrt(spread + EPS)


def norm_grad(centred, scale, grad):
    slope = jnp.mean(grad * centred, axis=-1, keepdims=True) * (scale * scale * scale)
    inner = grad * scale - centred * slope
    return inner - jnp.mean(inner, axis=-1, keepdims=True)


def kernel(
    tok_ref, wq_ref, wo_ref, go_ref,
    oq_ref, oc_ref,
    rows, extra, wq, wo, wpart, proj, gctx, hats, chances, bt, run, first,
    local, sent, g_recv, w_recv, y_recv, b_recv, r_recv,
):
    dp, mp = lax.axis_index("dp"), lax.axis_index("mp")
    z, yh = dp // 2, dp % 2
    x, yl, core = mp // 4, (mp // 2) % 2, mp % 2

    def place(z_, yh_, x_, yl_, core_):
        return (z_ * 2 + yh_, x_ * 4 + yl_ * 2 + core_)

    right_x, left_x, far_x = (x + 1) % NX, (x + 3) % NX, (x + 2) % NX
    pair = place(z, yh, x, 1 - yl, core)
    right = place(z, yh, right_x, yl, core)
    left = place(z, yh, left_x, yl, core)
    sibling = place(z, yh, x, yl, 1 - core)
    outer = place(z, 1 - yh, x, 1 - yl, core)
    across = place(z, 1 - yh, x, yl, core)
    up = place((z + 1) % NZ, yh, x, yl, core)
    down = place((z + 7) % NZ, yh, x, yl, core)
    sides = (up, down)

    def remote(src, dst, send, recv, to):
        return pltpu.make_async_remote_copy(
            src_ref=src, dst_ref=dst, send_sem=send, recv_sem=recv, device_id=to, device_id_type=MESH
        )

    barrier = pltpu.get_barrier_semaphore()
    for to in (pair, right, left, sibling, outer, across, up, down):
        pl.semaphore_signal(barrier, inc=1, device_id=to, device_id_type=MESH)

    mine = x * 2 + yl
    loads = (
        pltpu.make_async_copy(tok_ref, rows.at[0, mine, core], local.at[0]),
        pltpu.make_async_copy(go_ref, rows.at[1, mine, core], local.at[1]),
        pltpu.make_async_copy(wo_ref, wo.at[z, yh], local.at[2]),
        pltpu.make_async_copy(wq_ref, wq, local.at[3]),
    )
    for load in loads:
        load.start()
    proj[...] = jnp.zeros_like(proj)
    gctx[...] = jnp.zeros_like(gctx)
    for load in loads[:3]:
        load.wait()
    pl.semaphore_wait(barrier, 8)


    def target(r):
        j = r % NZ
        step = NZ // 2 - (j + 1) // 2
        return (z + jnp.where(j % 2 == 1, step, NZ - step)) % NZ

    def columns(r):
        return pl.ds(pl.multiple_of(target(r) * PAIR, PAIR), PAIR)

    def block(r, bx, by):
        return rows.at[r // NZ, bx * 2 + by, core, :, columns(r)]

    def move(r, slot, bx, by, to):
        part = block(r, bx, by)
        return remote(part, part, sent.at[0], g_recv.at[r, ARRIVES[slot]], to)

    def landed(r, slot, bx, by):
        move(r, slot, bx, by, pair).wait_recv()

    def landed_all(r, slot, count):
        part = rows.at[r // NZ, pl.ds(0, count), core, :, columns(r)]
        remote(part, part, sent.at[0], g_recv.at[r, ARRIVES[slot]], pair).wait_recv()

    def swap(r, lane):
        part = rows.at[r // NZ, :, lane, :, columns(r)]
        return remote(part, part, sent.at[1], g_recv.at[r, 4], sibling)

    def lend(r):
        cols = pl.ds(pl.multiple_of(target(r) * PAIR + (1 - yh) * SPAN, SPAN), SPAN)
        there = pl.ds(pl.multiple_of(target(r) * SPAN, SPAN), SPAN)
        half = pl.ds(core * 4, 4)
        return remote(
            rows.at[0, half, :, :, cols], extra.at[0, half, :, :, there],
            sent.at[2], g_recv.at[r, 5], outer,
        )

    def share(r, owner):
        there = pl.ds(pl.multiple_of(target(r) * SPAN, SPAN), SPAN)
        part = extra.at[0, pl.ds(owner * 4, 4), :, :, there]
        return remote(part, part, sent.at[3], g_recv.at[r, 6], sibling)

    def quarter(r, bx):
        there = pl.ds(pl.multiple_of(target(r) * SPAN, SPAN), SPAN)
        return extra.at[1, pl.ds(bx * 2, 2), core, :, there]

    def give(r):
        cols = pl.ds(pl.multiple_of(target(r) * PAIR + (1 - yh) * SPAN, SPAN), SPAN)
        mine = rows.at[1, pl.ds(x * 2, 2), core, :, cols]
        return remote(mine, quarter(r, x), sent.at[4], g_recv.at[r, 5], outer)

    def pass_quarter(r, slot, bx, to):
        part = quarter(r, bx)
        return remote(part, part, sent.at[5], g_recv.at[r, ARRIVES[slot]], to)

    def swap_quarters(r, lane):
        there = pl.ds(pl.multiple_of(target(r) * SPAN, SPAN), SPAN)
        part = extra.at[1, :, lane, :, there]
        return remote(part, part, sent.at[6], g_recv.at[r, 6], sibling)


    def weights(side, m):
        hop = m // 2
        from_z = (z + (NZ - hop if side == 0 else hop)) % NZ
        own = (m % 2 == 0) if (m < 6 or side == 0) else False
        part = wo.at[from_z, yh if own else 1 - yh]
        return remote(part, part, sent.at[7], w_recv.at[side, m], sides[side])

    def weights_landed(m):
        for side in range(2):
            weights(side, m).wait_recv()

    def weights_across():
        part = wo.at[z, yh]
        return remote(part, part, sent.at[8], y_recv.at[0], across)

    def send_weights(m):
        if m == 1:
            weights_across().wait_recv()
        if m >= 2:
            weights_landed(m - 2)
        if m == 6:
            weights_landed(5)
        for side in range(2):
            weights(side, m).start()


    def image_rows(i):
        return pl.ds(pl.multiple_of(i * PATCH, PATCH), PATCH)

    def head_part(i, h, part):
        return proj[image_rows(i), pl.ds(pl.multiple_of((h * 3 + part) * HD, HD), HD)]

    def sums(g, h):
        return pl.ds(pl.multiple_of((g * 2 + h) * HD, HD), HD)

    def hand_over(g, n):
        i, h = n // 2, n % 2
        return remote(
            bt.at[0, sums(g, h), image_rows(i)], bt.at[1, sums(g, h), image_rows(i)],
            sent.at[9], b_recv.at[g, n], across,
        )

    def forward(n):
        i, h = n // 2, n % 2
        centred_q, scale_q = centre(head_part(i, h, 0))
        centred_k, scale_k = centre(head_part(i, h, 1))
        query_hat = (centred_q * scale_q).astype(BF16)
        key_hat = (centred_k * scale_k).astype(BF16)
        value_hat = head_part(i, h, 2).astype(BF16)
        hats[n, 0] = query_hat
        hats[n, 1] = key_hat
        weight = jnp.exp(dot(query_hat, key_hat, ((1,), (1,))) * FACTOR)
        chance = weight / jnp.sum(weight, axis=-1, keepdims=True)
        chances[n] = chance
        context = dot(chance.astype(BF16), value_hat, ((1,), (0,)))
        bt[0, sums(3, h), image_rows(i)] = context.T.astype(BF16)
        hand_over(3, n).start()

    def backward(n):
        i, h = n // 2, n % 2
        chance = chances[n]
        chance_low = chance.astype(BF16)
        query_hat, key_hat = hats[n, 0], hats[n, 1]
        value_hat = head_part(i, h, 2).astype(BF16)
        grad_context = gctx[image_rows(i), pl.ds(pl.multiple_of(h * HD, HD), HD)].astype(BF16)
        grad_value = dot(chance_low, grad_context, ((0,), (0,)))
        bt[0, sums(0, h), image_rows(i)] = grad_value.T.astype(BF16)
        hand_over(0, n).start()
        grad_chance = dot(grad_context, value_hat, ((1,), (1,)))
        inner = jnp.sum(chance * grad_chance, axis=-1, keepdims=True)
        grad_score = (chance * (grad_chance - inner) * FACTOR).astype(BF16)
        grad_qhat = dot(grad_score, key_hat, ((1,), (0,)))
        grad_khat = dot(grad_score, query_hat, ((0,), (0,)))
        grad_key = norm_grad(*centre(head_part(i, h, 1)), grad_khat)
        bt[0, sums(1, h), image_rows(i)] = grad_key.T.astype(BF16)
        grad_query = norm_grad(*centre(head_part(i, h, 0)), grad_qhat)
        bt[0, sums(2, h), image_rows(i)] = grad_query.T.astype(BF16)

    def gathered(r):
        return rows[r // NZ, :, :, :, columns(r)].reshape(2 * PATCH, PAIR)

    def project(r):
        base = target(r) * PAIR

        @pl.loop(0, PAIR // HD)
        def _(k):
            here = pl.ds(pl.multiple_of(k * HD, HD), HD)
            wpart[here, :] = wq[pl.ds(pl.multiple_of(base + k * HD, HD), HD)].reshape(HD, 6 * HD)

        proj[...] += dot(gathered(r), wpart[...], ((1,), (0,)))

    def project_back(r):
        @pl.loop(0, PAIR // HD)
        def _(k):
            here = pl.ds(pl.multiple_of(k * HD, HD), HD)
            there = pl.ds(pl.multiple_of((k % 3) * HD, HD), HD)
            wpart[here, pl.ds(0, 2 * HD)] = wo[target(r), k // 3, there].reshape(HD, 2 * HD)

        gctx[...] += dot(gathered(r), wpart[:, pl.ds(0, 2 * HD)], ((1,), (0,)))


    def term(g, to_z):
        a = g // 3
        own_cols = pl.ds(pl.multiple_of(to_z * PAIR + yh * SPAN, SPAN), SPAN)
        other_cols = pl.ds(pl.multiple_of(to_z * SPAN, SPAN), SPAN)
        here = pl.ds(pl.multiple_of(g * 2 * HD, 2 * HD), 2 * HD)
        own = rows[a, :, :, :, own_cols].reshape(2 * PATCH, SPAN)
        other = extra[a, :, :, :, other_cols].reshape(2 * PATCH, SPAN)
        return dot(bt[0, here, :], own, ((1,), (0,))) + dot(bt[1, here, :], other, ((1,), (0,)))

    def chain(side, s, g, h):
        dp_to = ((z + jnp.where(side == 0, 1, 7)) % NZ) * 2 + yh
        return remote(
            run.at[side, s - 1, sums(g, h)], run.at[side, s, sums(g, h)],
            sent.at[10], r_recv.at[side, s, g * 2 + h], (dp_to, mp),
        )

    def chain_start(side, g, h):
        return remote(
            first.at[sums(g, h)], run.at[side, 0, sums(g, h)],
            sent.at[10], r_recv.at[side, 0, g * 2 + h], sides[side],
        )

    def chain_landed(side, s, g, h):
        part = run.at[side, s, sums(g, h)]
        remote(
            part, part, sent.at[10], r_recv.at[side, s, g * 2 + h], up
        ).wait_recv()

    def begin(g):
        part = term(g, (z + 4) % NZ)
        for h in range(2):
            first[sums(g, h)] = part[h * HD : (h + 1) * HD].astype(BF16)
            chain_start(h, g, h).start()

    def advance(g, side, s):
        part = term(g, (z + jnp.where(side == 0, 4 - s, 4 + s)) % NZ)
        for h in range(2):
            piece = part[h * HD : (h + 1) * HD]
            arrives = (s > 1) | (side == h)

            @pl.when(arrives)
            def _():
                chain_landed(side, s - 1, g, h)
                here = run[side, s - 1, sums(g, h)].astype(F32)
                run[side, s - 1, sums(g, h)] = (piece + here).astype(BF16)

            @pl.when(jnp.logical_not(arrives))
            def _():
                run[side, s - 1, sums(g, h)] = piece.astype(BF16)

            chain(side, s, g, h).start()

    def finish(g):
        total = term(g, z)
        for h in range(2):
            part = total[h * HD : (h + 1) * HD]
            for side in range(2):
                chain_landed(side, 3, g, h)
                part = part + run[side, 3, sums(g, h)].astype(F32)
            done = part.T.astype(BF16)

            @pl.when(g < 3)
            def _():
                oq_ref[:, pl.ds(pl.multiple_of((h * 3 + 2 - g) * HD, HD), HD)] = done

            @pl.when(g == 3)
            def _():
                oc_ref[:, h * HD : (h + 1) * HD] = done


    def stage(it, lag, least=0, most=ROUNDS):
        return pl.when((it - lag >= least) & (it - lag < most))

    weights_across().start()
    send_weights(0)

    @pl.loop(0, ROUNDS + 11)
    def _(it):
        @stage(it, 0)
        def _():
            move(it, 0, x, yl, pair).start()
            move(it, 1, x, yl, right).start()
            move(it, 2, x, yl, left).start()

        for m, when in ((1, 2), (2, 4), (3, 5), (4, 7), (5, 9), (6, 11)):

            @pl.when(it == when)
            def _(m=m):
                send_weights(m)

        @stage(it, 23, 0, 4)
        def _():
            backward(it - 23)

        @stage(it, 6)
        def _():
            r = it - 6
            landed_all(r, 3, 3)
            swap(r, core).start()

        @stage(it, 4)
        def _():
            r = it - 4
            landed(r, 5, far_x, yl)
            move(r, 6, far_x, yl, pair).start()

        @stage(it, 2)
        def _():
            r = it - 2
            landed(r, 0, x, 1 - yl)
            move(r, 3, x, 1 - yl, right).start()
            move(r, 4, x, 1 - yl, left).start()
            landed_all(r, 1, 2)
            onward = place(z, yh, jnp.where(core == 0, right_x, left_x), yl, core)
            move(r, 5, jnp.where(core == 0, left_x, right_x), yl, onward).start()

        @stage(it, 3, NZ)
        def _():
            give(it - 3).start()

        @stage(it, 5, NZ)
        def _():
            r = it - 5
            give(r).wait_recv()
            pass_quarter(r, 10, x, right).start()
            pass_quarter(r, 11, x, left).start()

        @stage(it, 7, NZ)
        def _():
            r = it - 7
            there = pl.ds(pl.multiple_of(target(r) * SPAN, SPAN), SPAN)
            both = extra.at[1, pl.ds(0, 4), core, :, there]
            remote(both, both, sent.at[5], g_recv.at[r, 7], right).wait_recv()
            onward = place(z, yh, jnp.where(core == 0, right_x, left_x), yl, core)
            pass_quarter(r, 12, jnp.where(core == 0, left_x, right_x), onward).start()

        @stage(it, 9, NZ)
        def _():
            r = it - 9
            pass_quarter(r, 12, far_x, right).wait_recv()
            swap_quarters(r, core).start()

        @pl.when((it >= 8) & (it < 24) & (it % 2 == 0))
        def _():
            lend((it - 8) // 2).start()

        @pl.when((it >= 11) & (it < 27) & (it % 2 == 1))
        def _():
            r = (it - 11) // 2
            lend(r).wait_recv()
            share(r, core).start()

        @pl.when(it == 7)
        def _():
            loads[3].wait()

        @pl.when(it == 15)
        def _():
            weights_landed(6)

        @stage(it, 7)
        def _():
            swap(it - 7, 1 - core).wait_recv()

        @stage(it, 7, 0, NZ)
        def _():
            project(it - 7)

        @stage(it, 7, NZ)
        def _():
            project_back(it - 7)

        @stage(it, 15, 0, 4)
        def _():
            forward(it - 15)

        @pl.when(it == 19)
        def _():
            for n in range(4):
                hand_over(3, n).wait_recv()

        @stage(it, 11, NZ)
        def _():
            r = it - 11
            j = r - NZ
            swap_quarters(r, 1 - core).wait_recv()

            @pl.when(j == 0)
            def _():
                begin(3)

            @pl.when((j > 0) & (j < 7))
            def _():
                advance(3, 1 - j % 2, (j + 1) // 2)

    @pl.loop(0, 4)
    def _(n):
        hand_over(1, n).start()

    @pl.loop(0, 4)
    def _(n):
        hand_over(2, n).start()

    @pl.loop(0, NZ)
    def _(r):
        share(r, 1 - core).wait_recv()

    def pick(t, table):
        return sum(jnp.where(t == i, v, 0) for i, v in enumerate(table) if v)

    plan = (
        (0, 0), (0, 1), (1, 0), (0, 2), (2, 0), (1, 1), (0, 3), (3, 4), (2, 1), (1, 2), (0, 4),
        (2, 2), (1, 3), (2, 3), (1, 4), (2, 4),
    )

    @pl.loop(0, len(plan))
    def _(t):
        g = pick(t, [g for g, _ in plan])
        s = pick(t, [s for _, s in plan])

        @pl.when(s == 0)
        def _():
            for n in range(4):
                hand_over(g, n).wait_recv()
            begin(g)

        @pl.when((s > 0) & (s < 4))
        def _():
            @pl.loop(0, 2)
            def _(side):
                advance(g, side, s)

        @pl.when(s == 4)
        def _():
            finish(g)


    gone = (
        rows.at[:, pl.ds(0, 7), core],
        rows.at[:, :, core],
        extra.at[0, pl.ds(0, 4)],
        extra.at[0, pl.ds(0, 4)],
        extra.at[1, pl.ds(0, 2), core],
        extra.at[1, pl.ds(0, 6), core],
        extra.at[1, :, core],
        wo.at[pl.ds(0, 7)],
        wo.at[0, 0],
        bt.at[0],
        run.at[:, :, pl.ds(0, 7 * HD)],
    )
    for kind, part in enumerate(gone):
        remote(part, part, sent.at[kind], y_recv.at[0], up).wait_send()


def split_heads(qkv_ref, out_ref, qkv_heads_ref, out_heads_ref):
    @pl.loop(0, SPAN // HD)
    def _(k):
        here = pl.ds(pl.multiple_of(k * HD, HD), HD)
        qkv_heads_ref[here] = qkv_ref[here].reshape(HD, 2, 3 * HD)
        out_heads_ref[here] = out_ref[here].reshape(HD, 2, HD)


def body(tokens, w_qkv, w_out, grad_out):
    dma = pltpu.SemaphoreType.DMA
    vmem = pltpu.VMEM
    grad_qkv, grad_wo = pl.pallas_call(
        kernel,
        out_shape=(
            jax.ShapeDtypeStruct((SPAN, 6 * HD), BF16),
            jax.ShapeDtypeStruct((SPAN, 2 * HD), BF16),
        ),
        in_specs=[pl.BlockSpec(memory_space=pl.ANY)] * 4,
        out_specs=(pl.BlockSpec(memory_space=vmem), pl.BlockSpec(memory_space=vmem)),
        scratch_shapes=[
            vmem((2, 8, 2, BLOCK, WIDTH), BF16),
            vmem((2, 8, 2, BLOCK, WIDTH // 2), BF16),
            vmem((WIDTH, 2, 3 * HD), BF16),
            vmem((NZ, 2, SPAN, 2, HD), BF16),
            vmem((PAIR, 6 * HD), BF16),
            vmem((2 * PATCH, 6 * HD), F32),
            vmem((2 * PATCH, 2 * HD), F32),
            vmem((4, 2, PATCH, HD), BF16),
            vmem((4, PATCH, PATCH), F32),
            vmem((2, 8 * HD, 2 * PATCH), BF16),
            vmem((2, 4, 8 * HD, SPAN), BF16),
            vmem((8 * HD, SPAN), BF16),
            dma((4,)),
            dma((11,)),
            dma((ROUNDS, 9)),
            dma((2, 7)),
            dma((1,)),
            dma((4, 4)),
            dma((2, 4, 8)),
        ],
        compiler_params=pltpu.CompilerParams(
            collective_id=0, has_side_effects=True, vmem_limit_bytes=60 << 20
        ),
    )(tokens, w_qkv, w_out, grad_out)
    return pl.pallas_call(
        split_heads,
        out_shape=(
            jax.ShapeDtypeStruct((SPAN, 2, 3 * HD), BF16),
            jax.ShapeDtypeStruct((SPAN, 2, HD), BF16),
        ),
        in_specs=[pl.BlockSpec(memory_space=vmem)] * 2,
        out_specs=(pl.BlockSpec(memory_space=vmem), pl.BlockSpec(memory_space=vmem)),
    )(grad_qkv, grad_wo)


def solution(mesh):
    return jax.shard_map(
        body,
        mesh=mesh,
        in_specs=(
            P(("dp", "mp"), None),
            P(None, "mp", None),
            P("dp", "mp", None),
            P(("dp", "mp"), None),
        ),
        out_specs=(P("dp", "mp", None), P("dp", "mp", None)),
        check_vma=False,
    )
```
